32 devices in a mesh: row: 8 (over y, x, core), col: 4 (over z).
Axes of the slice: x: 2, y: 2, z: 4, core: 2. Of those that a mesh axis runs over, the one named last changes fastest.
Arguments:
- factor_rows: float32 [512, 2, 2048], P(None, None, 'row'), may hold values from -0.00390625 to 0.00390625
- prev_solution: float32 [2048, 16384], P('row', 'col'), may hold values from -6 to 6
- cross_rows: float32 [512, 2, 16384], P('row', None, 'col'), may hold values from -0.2 to 0.2
- inverses: float32 [512, 2, 512], P('row'), as said below
- coupling: float32 [512, 512], P('row'), may hold values from -0.25 to 0.25
Outputs:
- downdate: float32 [16384, 16384], P('row', 'col')
The draws below stay inside these ranges and needn't reach their ends.
Inputs may be any that keep to these rules, and one draw needn't show every extreme that they name: Each block inverses[:, k, :] is lower triangular with a positive diagonal.
All inputs are finite; a program needn't handle non-finite values.
Results may differ from the reference program's by a relative error of at most 0.000096.
Values sent between devices are 32-bit elements; how exact they have to be, the bound alone decides.
No kernel may reach another device: no remote copies, remote signals or barrier semaphores. Data moves between devices by JAX's collectives and lax.ppermute only.
A program may use at most 128 MiB of HBM per device.

```python
import jax
import jax.numpy as jnp
from jax import lax

PANEL = 512
TESTS = 16384
SOLVED = 2048


def draw_inverses(key, part):
    inner = jax.random.fold_in(key, 11)
    key_low, key_diag = jax.random.split(inner)
    rows = jnp.arange(PANEL)[:, None, None]
    cols = jnp.arange(PANEL)[None, None, :]
    lower = jnp.clip(jax.random.normal(key_low, (PANEL, 2, PANEL), jnp.float32), -4.0, 4.0) * (0.8 / PANEL ** 0.5)
    diag = jax.random.uniform(key_diag, (PANEL, 2, 1), jnp.float32, 0.5, 1.5)
    return jnp.where(cols < rows, lower, jnp.where(cols == rows, diag, 0.0)).astype(jnp.float32)


def block_levels(stream_key, extent, shards, least, high):
    level = 1.0
    for axis_at, shards_of in shards:
        steps = jax.random.uniform(jax.random.fold_in(jax.random.fold_in(stream_key, 6), axis_at), (shards_of,), jnp.float32, least / len(shards), high / len(shards))
        level = level * jnp.repeat(jnp.exp(steps), extent[axis_at] // shards_of).reshape((-1,) + (1,) * (len(extent) - 1 - axis_at))
    return level


def normal_values(stream_key, shape, deviation, reach, cuts=(), held_as=jnp.bfloat16):
    entries = jax.random.normal(stream_key, shape, jnp.float32) * deviation
    if len(cuts) > 0:
        entries = block_levels(stream_key, shape, cuts, -0.22, 0.18) * entries
    return jnp.clip(entries, min=-reach, max=reach).astype(held_as)


def setup_inputs(seed: int = 0) -> dict:
    key_of = jax.random.split(jax.random.key(seed), 6)
    factor_rows = normal_values(key_of[0], (PANEL, 2, SOLVED), (SOLVED * 1024) ** -0.5, 0.00390625, ((2, 8),), jnp.float32)
    prev_solution = normal_values(key_of[1], (SOLVED, TESTS), 1.0, 6.0, ((0, 8), (1, 4)), jnp.float32)
    cross_rows = normal_values(key_of[2], (PANEL, 2, TESTS), 0.03125, 0.2, ((0, 8), (2, 4)), jnp.float32)
    inverses = draw_inverses(jax.random.fold_in(key_of[5], 71), 0)
    coupling = normal_values(key_of[4], (PANEL, PANEL), PANEL ** -0.5, 0.25, ((0, 8),), jnp.float32)
    return {"factor_rows": factor_rows, "prev_solution": prev_solution, "cross_rows": cross_rows, "inverses": inverses, "coupling": coupling}


def reference(factor_rows, prev_solution, cross_rows, inverses, coupling):
    full = lax.Precision.HIGHEST
    update = cross_rows - jnp.einsum("pks,sn->pkn", factor_rows, prev_solution, precision=full, preferred_element_type=jnp.float32)
    first = jnp.dot(inverses[:, 0, :], update[:, 0, :], precision=full, preferred_element_type=jnp.float32)
    rest = update[:, 1, :] - jnp.dot(coupling, first, precision=full, preferred_element_type=jnp.float32)
    second = jnp.dot(inverses[:, 1, :], rest, precision=full, preferred_element_type=jnp.float32)
    solved = jnp.concatenate([first, second], axis=0)
    return jnp.dot(solved.T, solved, precision=full, preferred_element_type=jnp.float32)
```

```python
import functools

import jax
import jax.numpy as jnp
from jax import lax
from jax.experimental import pallas as pl
from jax.experimental.pallas import tpu as pltpu
from jax.sharding import PartitionSpec as P

def dot(a, b, precision=lax.Precision.HIGHEST):
    return jnp.dot(a, b, precision=precision, preferred_element_type=jnp.float32)


def halves(x):
    high = x.astype(jnp.bfloat16)
    return high, (x - high.astype(jnp.float32)).astype(jnp.bfloat16)


def product(a, b, contract=1):
    return lax.dot_general(
        a, b, (((contract,), (0,)), ((), ())), preferred_element_type=jnp.float32
    )


def three(a, b, contract=1):
    (a_high, a_low), (b_high, b_low) = a, b
    small = product(a_high, b_low, contract) + product(a_low, b_high, contract)
    return product(a_high, b_high, contract) + small


def cost(flops, moved):
    return pl.CostEstimate(flops=flops, bytes_accessed=moved, transcendentals=0)


def roomy(limit=56):
    return pltpu.CompilerParams(vmem_limit_bytes=limit << 20)


def corner_kernel(table, *outs):
    depth = table.shape[0] * table.shape[2]
    first, second, couple = [halves(table[:, n].reshape(depth, -1)) for n in range(3)]
    corner = -three(second, halves(three(couple, first)))
    outs[0][...], outs[1][...] = first
    outs[2][...], outs[3][...] = halves(corner)
    outs[4][...], outs[5][...] = second


def transfer_matrix(inverses, coupling):
    table = jnp.concatenate([jnp.swapaxes(inverses, 0, 1), coupling[None]], axis=0)
    table = lax.all_gather(table, "row", axis=0)
    panel = coupling.shape[1]
    return pl.pallas_call(
        corner_kernel,
        out_shape=[jax.ShapeDtypeStruct((panel, panel), jnp.bfloat16)] * 6,
        compiler_params=roomy(),
        cost_estimate=cost(12 * panel**3, 24 * panel**2),
    )(table)


def partial_updates(steps, info, f_own, f_given, p_own, p_given, c_own, c_given, *refs):
    outs, (f_high, f_low) = refs[:-2], refs[-2:]
    step = pl.program_id(0)
    depth, span = f_own.shape
    near = c_own.shape[1]

    @pl.when(step == 0)
    def _():
        for side, part in enumerate((f_own, f_given)):
            cut = slice(side * span, (side + 1) * span)
            f_high[:, cut], f_low[:, cut] = halves(part[...])

    columns = jnp.concatenate([p_own[...], p_given[...]], axis=0)
    total = -three((f_high[...], f_low[...]), halves(columns))
    for n, parts in enumerate(steps):

        @pl.when(step == n)
        def _(parts=parts):
            for out, start, taken, size in parts:
                into, cut = slice(start, start + size), slice(taken, taken + size)
                outs[out][:, into] = total[:, cut]
                for part, rank in ((c_own, info[-2]), (c_given, info[-1])):
                    for k in range(2):
                        rows = pl.ds(pl.multiple_of(k * (depth // 2) + rank * near, near), near)
                        outs[out][rows, into] = outs[out][rows, into] + part[k][:, cut]


def update_blocks(info, steps, widths, sources):
    f_own, _, p_own, _, c_own, _ = sources
    depth, span = f_own.shape
    near = c_own.shape[1]
    wide = p_own.shape[1] // 16
    count = len(steps)
    own = lambda i, info: info[count] * 8 + info[i]
    return pl.pallas_call(
        lambda info, *refs: partial_updates(
            steps, [info[count + n] for n in range(3)], *refs
        ),
        grid_spec=pltpu.PrefetchScalarGridSpec(
            num_scalar_prefetch=1,
            grid=(count,),
            in_specs=[
                pl.BlockSpec((depth, span), lambda i, info: (0, 0)),
                pl.BlockSpec((depth, span), lambda i, info: (0, 0)),
                pl.BlockSpec((span, wide), lambda i, info: (0, own(i, info))),
                pl.BlockSpec((span, wide), lambda i, info: (0, info[i])),
                pl.BlockSpec((2, near, wide), lambda i, info: (0, 0, own(i, info))),
                pl.BlockSpec((2, near, wide), lambda i, info: (0, 0, info[i])),
            ],
            out_specs=[pl.BlockSpec((depth, w), lambda i, info: (0, 0)) for w in widths],
            scratch_shapes=[pltpu.VMEM((depth, 2 * span), jnp.bfloat16)] * 2,
        ),
        out_shape=[jax.ShapeDtypeStruct((depth, w), jnp.float32) for w in widths],
        compiler_params=roomy(),
        cost_estimate=cost(
            6 * depth * 2 * span * count * wide, 4 * depth * (2 * span + count * wide)
        ),
    )(info, *sources)


def solve_kernel(*refs):
    matrix, (keep, a_got, b_got, a_last, b_last) = refs[:6], refs[6:11]
    solved, chunks = refs[11], refs[12:]
    panel, half = keep.shape[0] // 2, a_last.shape[1]
    arrived = [
        got[:, half:] + last[...] for got, last in ((a_got, a_last), (b_got, b_last))
    ]
    update = keep[...] + jnp.concatenate(arrived, axis=1)
    upper, lower = halves(update[:panel]), halves(update[panel:])
    first, corner, second = [(matrix[n][...], matrix[n + 1][...]) for n in (0, 2, 4)]
    top = three(first, upper)
    low = three(corner, upper) + three(second, lower)
    solved[:panel, :] = top
    solved[panel:, :] = low
    for n, chunk in enumerate(chunks):
        cut = slice(n * chunk.shape[1], (n + 1) * chunk.shape[1])
        chunk[:panel, :] = top[:, cut]
        chunk[panel:, :] = low[:, cut]


def solve(matrix, terms, widths, whole):
    panel = matrix[0].shape[0]
    depth, wide = terms[0].shape
    shape = lambda w: jax.ShapeDtypeStruct((depth, w), jnp.float32)
    full = lambda x: pl.BlockSpec(x.shape, lambda i: (0, 0))
    ins = [*matrix, *terms]
    kernel, specs, side, aliases = solve_kernel, [full(x) for x in ins], 0, {}
    if whole is not None:
        kernel = lambda *refs: solve_kernel(*refs[:11], *refs[12:])
        specs, side, aliases = [*specs, pl.BlockSpec(memory_space=pl.ANY)], 1, {11: 0}
        ins = [*ins, whole]
    return pl.pallas_call(
        kernel,
        grid=(1,),
        in_specs=specs,
        out_specs=[pl.BlockSpec((depth, wide), lambda i: (0, side))]
        + [pl.BlockSpec((depth, w), lambda i: (0, 0)) for w in widths],
        out_shape=[shape(2 * wide)] + [shape(w) for w in widths],
        input_output_aliases=aliases,
        compiler_params=roomy(),
        cost_estimate=cost(18 * panel * panel * wide, 4 * (3 * panel**2 + 6 * depth * wide)),
    )(*ins)


def split_kernel(parts, place, *refs):
    del place
    high, low = refs[-2:]
    for m in range(4):

        @pl.when(pl.program_id(0) // parts == m)
        def _(block=refs[m]):
            high[0], low[0] = halves(block[...])


def split_blocks(place, blocks, held):
    depth, width = blocks[0].shape
    parts = 2
    rows = depth // parts
    shape = jax.ShapeDtypeStruct((8, depth, width), jnp.bfloat16)
    spec = pl.BlockSpec((1, rows, width), lambda i, place: (place[i // parts], i % parts, 0))

    def taken(m):
        return pl.BlockSpec(
            (rows, width), lambda i, place: (jnp.clip(i - parts * m, 0, parts - 1), 0)
        )

    held = list(held)
    return pl.pallas_call(
        functools.partial(split_kernel, parts),
        grid_spec=pltpu.PrefetchScalarGridSpec(
            num_scalar_prefetch=1,
            grid=(4 * parts,),
            in_specs=[taken(m) for m in range(4)]
            + [pl.BlockSpec(memory_space=pl.ANY)] * len(held),
            out_specs=[spec, spec],
        ),
        out_shape=[shape, shape],
        input_output_aliases={5: 0, 6: 1} if held else {},
        compiler_params=roomy(40),
        cost_estimate=cost(0, 8 * 4 * depth * width),
    )(place, *blocks, *held)


def downdate_kernel(info, mine, *refs):
    others, gathered = refs[:3], refs[3:6]
    high, low = refs[6:8]
    out, left_high, left_low = refs[-3:]
    width = others[0].shape[1]

    @pl.when(pl.program_id(0) == 0)
    def _():
        inside = info[1] == 1
        pieces = [mine[0]] + [
            jnp.where(inside, own[...], other[...]) for other, own in zip(others, gathered)
        ]
        for m, piece in enumerate(pieces):
            cut = slice(m * width, (m + 1) * width)
            left_high[:, cut], left_low[:, cut] = halves(piece)

    total = three((left_high[...], left_low[...]), (high[0], low[0]), 0)
    for m in range(4):
        out[info[0] ^ m] = total[m * width : (m + 1) * width]


def downdate_part(info, blocks, others, gathered, held, out, at):
    _, depth, width = blocks.shape
    wide = held[0].shape[2]
    rows = 4 * width
    specs = [pl.BlockSpec((1, depth, width), lambda j, info: (info[0], 0, 0))]
    specs += [pl.BlockSpec((depth, width), lambda j, info: (0, 0))] * 3
    specs += [pl.BlockSpec((depth, width), lambda j, info: (0, at))] * 3
    specs += [pl.BlockSpec((1, depth, wide), lambda j, info: (j, 0, 0))] * 2
    ins = [blocks, *others, *gathered, *held]
    aliases = {}
    if out is not None:
        specs += [pl.BlockSpec(memory_space=pl.ANY)]
        ins += [out]
        aliases = {len(ins): 0}
    return pl.pallas_call(
        downdate_kernel,
        grid_spec=pltpu.PrefetchScalarGridSpec(
            num_scalar_prefetch=1,
            grid=(8,),
            in_specs=specs,
            out_specs=pl.BlockSpec((4, width, wide), lambda j, info: (0, at, j)),
            scratch_shapes=[pltpu.VMEM((depth, rows), jnp.bfloat16)] * 2,
        ),
        out_shape=jax.ShapeDtypeStruct((4, wide, 8 * wide), jnp.float32),
        input_output_aliases=aliases,
        compiler_params=roomy(),
        cost_estimate=cost(
            6 * depth * rows * 8 * wide, 4 * (2 * depth * rows + 8 * depth * wide + rows * 8 * wide)
        ),
    )(info, *ins)


CORE = [(i, i ^ 1) for i in range(8)]
ALONG_X = [(i, i ^ 2) for i in range(8)]
ALONG_Y = [(i, i ^ 4) for i in range(8)]


def to_others(across):
    return [
        ((j * 2 + c) * 4 + z, ((j ^ across) * 2 + c) * 4 + z)
        for j in range(4)
        for c in range(2)
        for z in range(4)
        if j ^ across != z
    ]


def after(x, *others):
    return lax.optimization_barrier((x, *others))[0]


def local(factor_rows, prev_solution, cross_rows, inverses, coupling):
    rank, plane = lax.axis_index("row"), lax.axis_index("col")
    chip, core = rank // 2, rank % 2
    depth = 2 * factor_rows.shape[0]
    width = prev_solution.shape[1]
    half, quarter = width // 16, width // 32
    ints = lambda *values: jnp.stack([jnp.asarray(v, jnp.int32) for v in values])

    matrix = transfer_matrix(inverses, coupling)
    there = lambda x: lax.dynamic_slice_in_dim(
        x, (1 - core) * (width // 2), width // 2, x.ndim - 1
    )
    p_given = lax.ppermute(there(prev_solution), "row", CORE)
    c_own = jnp.swapaxes(cross_rows, 0, 1)
    c_given = lax.ppermute(there(c_own), "row", CORE)
    f_own = jnp.swapaxes(factor_rows, 0, 1).reshape(depth, -1)
    f_given = lax.ppermute(f_own, "row", CORE)
    sources = (f_own, f_given, prev_solution, p_given, c_own, c_given)

    away = (
        ((0, 0, 0, quarter), (1, 0, quarter, quarter)),
        ((0, quarter, 0, quarter), (3, 0, quarter, quarter)),
        ((2, 0, 0, quarter), (1, quarter, quarter, quarter)),
    )
    away_widths = (half, half, quarter, quarter)

    def updates(places, steps, widths):
        spots = [(chip ^ across) * 2 + side for across, side in places]
        return update_blocks(ints(*spots, core, rank, rank ^ 1), steps, widths, sources)

    def arrivals(a_out, b_out, a_on, b_on):
        a_got = lax.ppermute(a_out, "row", ALONG_X)
        b_got = lax.ppermute(b_out, "row", ALONG_Y)
        a_on, b_on = a_on + a_got[:, :quarter], b_on + b_got[:, :quarter]
        a_last = lax.ppermute(a_on, "row", ALONG_Y)
        b_last = lax.ppermute(b_on, "row", ALONG_X)
        return (a_got, b_got, a_last, b_last), a_on

    early = updates(((3, 0), (1, 0), (2, 0)), away, away_widths)
    *late, keep, late_keep = updates(
        ((3, 1), (1, 1), (2, 1), (0, 0), (0, 1)),
        (*away, ((4, 0, 0, half),), ((5, 0, 0, half),)),
        (*away_widths, half, half),
    )
    terms, sent = arrivals(*early)
    solved, chunk = solve(matrix, (keep, *terms), (half,), None)
    late = [after(x, sent) for x in late[:2]] + late[2:]
    terms, _ = arrivals(*late)
    solved, *chunks = solve(matrix, (late_keep, *terms), (quarter, quarter), solved)
    blocks = [lax.all_gather(x, "col", axis=0) for x in (chunk, *chunks)]

    from_x = lax.ppermute(solved, "row", ALONG_X)
    from_y = lax.ppermute(solved, "row", ALONG_Y)
    far_a = lax.ppermute(from_x[:, :half], "row", ALONG_Y)
    far_b = lax.ppermute(from_y[:, half:], "row", ALONG_X)
    far = jnp.concatenate([far_a, far_b], axis=1)
    gathered = [solved, from_x, from_y, far]
    held = split_blocks(ints(*[core * 4 + (chip ^ m) for m in range(4)]), gathered, ())
    given = [lax.ppermute(block, "row", CORE) for block in gathered]
    held = split_blocks(ints(*[(1 - core) * 4 + (chip ^ m) for m in range(4)]), given, held)

    info = ints(chip, chip == plane)
    out = None
    for block, at in zip(blocks, (0, 2, 3)):
        others = [
            lax.ppermute(
                lax.dynamic_index_in_dim(block, chip ^ m, 0, keepdims=False),
                ("row", "col"),
                to_others(m),
            )
            for m in (1, 2, 3)
        ]
        out = downdate_part(info, block, others, gathered[1:], held, out, at)
    return out.reshape(-1, width)


def local_any(factor_rows, prev_solution, cross_rows, inverses, coupling):
    full = lax.Precision.HIGHEST
    width = prev_solution.shape[1]
    fanout = lax.axis_size("row") // lax.axis_size("col")
    narrow = width // fanout
    rank = lax.axis_index("row")
    sums = lax.psum_scatter(
        jnp.einsum(
            "pks,sn->pkn",
            factor_rows,
            prev_solution,
            precision=full,
            preferred_element_type=jnp.float32,
        ),
        "row",
        scatter_dimension=0,
        tiled=True,
    )
    update = lax.all_gather(cross_rows - sums, "row", axis=0, tiled=True)
    lower = lax.all_gather(inverses, "row", axis=0, tiled=True)
    couple = lax.all_gather(coupling, "row", axis=0, tiled=True)
    first = dot(lower[:, 0, :], update[:, 0, :], full)
    rest = update[:, 1, :] - dot(couple, first, full)
    second = dot(lower[:, 1, :], rest, full)
    stacked = jnp.concatenate([first, second], axis=0)
    cut = lax.dynamic_slice_in_dim(stacked, rank % fanout * narrow, narrow, 1)
    mine = lax.axis_index("col") == rank // fanout
    picked = lax.psum(jnp.where(mine, cut, jnp.zeros_like(cut)), "col")
    return lax.dot_general(
        picked, stacked, (((0,), (0,)), ((), ())), precision=full, preferred_element_type=jnp.float32
    )


def solution(mesh):
    body = local if (mesh.shape["row"], mesh.shape["col"]) == (8, 4) else local_any
    return jax.shard_map(
        body,
        mesh=mesh,
        in_specs=(
            P(None, None, "row"),
            P("row", "col"),
            P("row", None, "col"),
            P("row", None, None),
            P("row", None),
        ),
        out_specs=P("row", "col"),
        check_vma=False,
    )
```

```python
import functools

import jax
import jax.numpy as jnp
from jax import lax
from jax.experimental import pallas as pl
from jax.experimental.pallas import tpu as pltpu
from jax.sharding import PartitionSpec as P

def dot(a, b, precision=lax.Precision.HIGHEST):
    return jnp.dot(a, b, precision=precision, preferred_element_type=jnp.float32)


def halves(x):
    high = x.astype(jnp.bfloat16)
    return high, (x - high.astype(jnp.float32)).astype(jnp.bfloat16)


def product(a, b, contract=1):
    return lax.dot_general(
        a, b, (((contract,), (0,)), ((), ())), preferred_element_type=jnp.float32
    )


def three(a, b, contract=1):
    (a_high, a_low), (b_high, b_low) = a, b
    small = product(a_high, b_low, contract) + product(a_low, b_high, contract)
    return product(a_high, b_high, contract) + small


def cost(flops, moved):
    return pl.CostEstimate(flops=flops // 32, bytes_accessed=moved // 32, transcendentals=0)


def roomy(limit=56):
    return pltpu.CompilerParams(vmem_limit_bytes=limit << 20)


def corner_kernel(table, *outs):
    depth = table.shape[0] * table.shape[2]
    first, second, couple = [halves(table[:, n].reshape(depth, -1)) for n in range(3)]
    corner = -three(second, halves(three(couple, first)))
    outs[0][...], outs[1][...] = first
    outs[2][...], outs[3][...] = halves(corner)
    outs[4][...], outs[5][...] = second


def transfer_matrix(inverses, coupling):
    table = jnp.concatenate([jnp.swapaxes(inverses, 0, 1), coupling[None]], axis=0)
    table = lax.all_gather(table, "row", axis=0)
    panel = coupling.shape[1]
    return pl.pallas_call(
        corner_kernel,
        out_shape=[jax.ShapeDtypeStruct((panel, panel), jnp.bfloat16)] * 6,
        compiler_params=roomy(),
        cost_estimate=cost(12 * panel**3, 24 * panel**2),
    )(table)


def partial_updates(steps, info, f_own, f_given, p_own, p_given, c_own, c_given, *refs):
    outs, (f_high, f_low) = refs[:-2], refs[-2:]
    step = pl.program_id(0)
    depth, span = f_own.shape
    near = c_own.shape[1]

    @pl.when(step == 0)
    def _():
        for side, part in enumerate((f_own, f_given)):
            cut = slice(side * span, (side + 1) * span)
            f_high[:, cut], f_low[:, cut] = halves(part[...])

    columns = jnp.concatenate([p_own[...], p_given[...]], axis=0)
    total = -three((f_high[...], f_low[...]), halves(columns))
    for n, parts in enumerate(steps):

        @pl.when(step == n)
        def _(parts=parts):
            for out, start, taken, size in parts:
                into, cut = slice(start, start + size), slice(taken, taken + size)
                outs[out][:, into] = total[:, cut]
                for part, rank in ((c_own, info[-2]), (c_given, info[-1])):
                    for k in range(2):
                        rows = pl.ds(pl.multiple_of(k * (depth // 2) + rank * near, near), near)
                        outs[out][rows, into] = outs[out][rows, into] + part[k][:, cut]


def update_blocks(info, steps, widths, sources):
    f_own, _, p_own, _, c_own, _ = sources
    depth, span = f_own.shape
    near = c_own.shape[1]
    wide = p_own.shape[1] // 16
    count = len(steps)
    own = lambda i, info: info[count] * 8 + info[i]
    return pl.pallas_call(
        lambda info, *refs: partial_updates(
            steps, [info[count + n] for n in range(3)], *refs
        ),
        grid_spec=pltpu.PrefetchScalarGridSpec(
            num_scalar_prefetch=1,
            grid=(count,),
            in_specs=[
                pl.BlockSpec((depth, span), lambda i, info: (0, 0)),
                pl.BlockSpec((depth, span), lambda i, info: (0, 0)),
                pl.BlockSpec((span, wide), lambda i, info: (0, own(i, info))),
                pl.BlockSpec((span, wide), lambda i, info: (0, info[i])),
                pl.BlockSpec((2, near, wide), lambda i, info: (0, 0, own(i, info))),
                pl.BlockSpec((2, near, wide), lambda i, info: (0, 0, info[i])),
            ],
            out_specs=[pl.BlockSpec((depth, w), lambda i, info: (0, 0)) for w in widths],
            scratch_shapes=[pltpu.VMEM((depth, 2 * span), jnp.bfloat16)] * 2,
        ),
        out_shape=[jax.ShapeDtypeStruct((depth, w), jnp.float32) for w in widths],
        compiler_params=roomy(),
        cost_estimate=cost(
            6 * depth * 2 * span * count * wide, 4 * depth * (2 * span + count * wide)
        ),
    )(info, *sources)


def solve_kernel(*refs):
    matrix, (keep, a_got, b_got, a_last, b_last) = refs[:6], refs[6:11]
    solved, chunks = refs[11], refs[12:]
    panel, half = keep.shape[0] // 2, a_last.shape[1]
    arrived = [
        got[...] + last[...] for got, last in ((a_got, a_last), (b_got, b_last))
    ]
    update = keep[...] + jnp.concatenate(arrived, axis=1)
    upper, lower = halves(update[:panel]), halves(update[panel:])
    first, corner, second = [(matrix[n][...], matrix[n + 1][...]) for n in (0, 2, 4)]
    top = three(first, upper)
    low = three(corner, upper) + three(second, lower)
    solved[:panel, :] = top
    solved[panel:, :] = low
    for n, chunk in enumerate(chunks):
        cut = slice(n * chunk.shape[1], (n + 1) * chunk.shape[1])
        chunk[:panel, :] = top[:, cut]
        chunk[panel:, :] = low[:, cut]


def solve(matrix, terms, widths, whole):
    panel = matrix[0].shape[0]
    depth, wide = terms[0].shape
    shape = lambda w: jax.ShapeDtypeStruct((depth, w), jnp.float32)
    full = lambda x: pl.BlockSpec(x.shape, lambda i: (0, 0))
    ins = [*matrix, *terms]
    kernel, specs, side, aliases = solve_kernel, [full(x) for x in ins], 0, {}
    if whole is not None:
        kernel = lambda *refs: solve_kernel(*refs[:11], *refs[12:])
        specs, side, aliases = [*specs, pl.BlockSpec(memory_space=pl.ANY)], 1, {11: 0}
        ins = [*ins, whole]
    return pl.pallas_call(
        kernel,
        grid=(1,),
        in_specs=specs,
        out_specs=[pl.BlockSpec((depth, wide), lambda i: (0, side))]
        + [pl.BlockSpec((depth, w), lambda i: (0, 0)) for w in widths],
        out_shape=[shape(2 * wide)] + [shape(w) for w in widths],
        input_output_aliases=aliases,
        compiler_params=roomy(),
        cost_estimate=cost(18 * panel * panel * wide, 4 * (3 * panel**2 + 6 * depth * wide)),
    )(*ins)


def split_kernel(parts, count, place, *refs):
    del place
    high, low = refs[-2:]
    for m in range(count):

        @pl.when(pl.program_id(0) // parts == m)
        def _(block=refs[m]):
            high[0], low[0] = halves(block[...])


def split_blocks(place, blocks, held, weight=1):
    depth, width = blocks[0].shape
    count, parts = len(blocks), 2
    rows = depth // parts
    shape = jax.ShapeDtypeStruct((8, depth, width), jnp.bfloat16)
    spec = pl.BlockSpec((1, rows, width), lambda i, place: (place[i // parts], i % parts, 0))

    def taken(m):
        return pl.BlockSpec(
            (rows, width), lambda i, place: (jnp.clip(i - parts * m, 0, parts - 1), 0)
        )

    held = list(held)
    return pl.pallas_call(
        functools.partial(split_kernel, parts, count),
        grid_spec=pltpu.PrefetchScalarGridSpec(
            num_scalar_prefetch=1,
            grid=(count * parts,),
            in_specs=[taken(m) for m in range(count)]
            + [pl.BlockSpec(memory_space=pl.ANY)] * len(held),
            out_specs=[spec, spec],
        ),
        out_shape=[shape, shape],
        input_output_aliases={count + 1: 0, count + 2: 1} if held else {},
        compiler_params=roomy(),
        cost_estimate=cost(0, 8 * count * depth * width * weight),
    )(place, *blocks, *held)


def downdate_kernel(pieces, high, low, *refs):
    out, left_high, left_low = refs[-3:]
    count, _, width = pieces.shape

    @pl.when(pl.program_id(0) == 0)
    def _():
        for j in range(count):
            cut = slice(j * width, (j + 1) * width)
            left_high[:, cut], left_low[:, cut] = halves(pieces[j])

    total = three((left_high[...], left_low[...]), (high[0], low[0]), 0)
    for j in range(count):
        out[j] = total[j * width : (j + 1) * width]


def downdate_part(pieces, held, out, at):
    count, depth, width = pieces.shape
    wide = held[0].shape[2]
    rows = count * width
    specs = [pl.BlockSpec((count, depth, width), lambda j: (0, 0, 0))]
    specs += [pl.BlockSpec((1, depth, wide), lambda j: (j, 0, 0))] * 2
    ins = [pieces, *held]
    aliases = {}
    if out is not None:
        specs += [pl.BlockSpec(memory_space=pl.ANY)]
        ins += [out]
        aliases = {3: 0}
    return pl.pallas_call(
        downdate_kernel,
        grid=(8,),
        in_specs=specs,
        out_specs=pl.BlockSpec((count, width, wide), lambda j: (0, at, j)),
        out_shape=jax.ShapeDtypeStruct((count, wide, 8 * wide), jnp.float32),
        scratch_shapes=[pltpu.VMEM((depth, rows), jnp.bfloat16)] * 2,
        input_output_aliases=aliases,
        compiler_params=roomy(),
        cost_estimate=cost(
            6 * depth * rows * 8 * wide, 4 * (depth * rows + 8 * depth * wide + rows * 8 * wide)
        ),
    )(*ins)


CORE = [(i, i ^ 1) for i in range(8)]
ALONG_X = [(i, i ^ 2) for i in range(8)]
ALONG_Y = [(i, i ^ 4) for i in range(8)]


SAME_CORE = [[0, 2, 4, 6], [1, 3, 5, 7]]


def to_chips(blocks):
    return lax.all_to_all(blocks, "row", 0, 0, axis_index_groups=SAME_CORE)


def after(x, *others):
    return lax.optimization_barrier((x, *others))[0]


def local(factor_rows, prev_solution, cross_rows, inverses, coupling):
    rank, plane = lax.axis_index("row"), lax.axis_index("col")
    chip, core = rank // 2, rank % 2
    depth = 2 * factor_rows.shape[0]
    width = prev_solution.shape[1]
    half, quarter = width // 16, width // 32
    ints = lambda *values: jnp.stack([jnp.asarray(v, jnp.int32) for v in values])

    matrix = transfer_matrix(inverses, coupling)
    there = lambda x: lax.dynamic_slice_in_dim(
        x, (1 - core) * (width // 2), width // 2, x.ndim - 1
    )
    p_given = lax.ppermute(there(prev_solution), "row", CORE)
    c_own = jnp.swapaxes(cross_rows, 0, 1)
    c_given = lax.ppermute(there(c_own), "row", CORE)
    f_own = jnp.swapaxes(factor_rows, 0, 1).reshape(depth, -1)
    f_given = lax.ppermute(f_own, "row", CORE)
    sources = (f_own, f_given, prev_solution, p_given, c_own, c_given)

    away = (
        ((0, 0, 0, quarter), (1, 0, quarter, quarter)),
        ((2, 0, 0, quarter), (5, 0, quarter, quarter)),
        ((4, 0, 0, quarter), (3, 0, quarter, quarter)),
    )

    def updates(places, steps, widths):
        spots = [(chip ^ across) * 2 + side for across, side in places]
        return update_blocks(ints(*spots, core, rank, rank ^ 1), steps, widths, sources)

    early = updates(((3, 0), (1, 0), (2, 0)), away, (quarter,) * 6)
    *late, keep, late_keep = updates(
        ((3, 1), (1, 1), (2, 1), (0, 0), (0, 1)),
        (*away, ((6, 0, 0, half),), ((7, 0, 0, half),)),
        (*(quarter,) * 6, half, half),
    )

    def passed(a_pass, b_pass):
        return lax.ppermute(a_pass, "row", ALONG_X), lax.ppermute(b_pass, "row", ALONG_Y)

    def arrivals(first, a_send, b_send, a_on, b_on):
        a_got, b_got = passed(a_send, b_send)
        a_last = lax.ppermute(a_on + first[0], "row", ALONG_Y)
        b_last = lax.ppermute(b_on + first[1], "row", ALONG_X)
        return a_got, b_got, a_last, b_last

    first = passed(*early[:2])
    first = after(first[0], late_keep, matrix[0]), first[1]
    terms = arrivals(first, *early[2:])
    first = passed(*[after(x, terms[0]) for x in late[:2]])
    solved, chunk = solve(matrix, (keep, *terms), (half,), None)
    late_terms = arrivals(first, *late[2:])
    solved, *chunks = solve(matrix, (late_keep, *late_terms), (quarter, quarter), solved)
    blocks = [lax.all_gather(x, "col", axis=0) for x in (chunk, *chunks)]

    from_x = lax.ppermute(solved, "row", ALONG_X)
    from_y = lax.ppermute(solved, "row", ALONG_Y)
    twin = lax.ppermute(solved, "row", CORE)

    def split(blocks, pair, group, held, weight=1):
        places = [c * 4 + (chip ^ m) for c in (core, 1 - core) for m in group]
        return split_blocks(ints(*places), [*blocks, *pair], held, weight)

    def given(*arrays):
        return [lax.ppermute(x, "row", CORE) for x in arrays]

    held = split([solved], [twin], (0,), ())
    first_chunk = blocks[0][:, :, :quarter]
    from_x, from_y = after(from_x, first_chunk, *held), after(from_y, first_chunk, *held)
    far_a = lax.ppermute(from_x[:, :half], "row", ALONG_Y)
    far_b = lax.ppermute(from_y[:, half:], "row", ALONG_X)

    held = split([from_x, from_y], given(from_x, from_y), (1, 2), held)
    far = jnp.concatenate([after(far_a, *held), far_b], axis=1)
    pieces = to_chips(first_chunk)
    twin = given(far)
    held = split([after(far, pieces, blocks[1])], twin, (3,), held)
    out = before = downdate_part(pieces, held, None, 0)
    pieces = to_chips(blocks[0][:, :, quarter:])
    out = downdate_part(pieces, held, out, 1)
    pieces = to_chips(after(blocks[1], before))
    before, out = out, downdate_part(pieces, held, out, 2)
    pieces = to_chips(after(blocks[2], before))
    out = downdate_part(pieces, held, out, 3)
    return out.reshape(-1, width)


def local_any(factor_rows, prev_solution, cross_rows, inverses, coupling):
    full = lax.Precision.HIGHEST
    width = prev_solution.shape[1]
    fanout = lax.axis_size("row") // lax.axis_size("col")
    narrow = width // fanout
    rank = lax.axis_index("row")
    sums = lax.psum_scatter(
        jnp.einsum(
            "pks,sn->pkn",
            factor_rows,
            prev_solution,
            precision=full,
            preferred_element_type=jnp.float32,
        ),
        "row",
        scatter_dimension=0,
        tiled=True,
    )
    update = lax.all_gather(cross_rows - sums, "row", axis=0, tiled=True)
    lower = lax.all_gather(inverses, "row", axis=0, tiled=True)
    couple = lax.all_gather(coupling, "row", axis=0, tiled=True)
    first = dot(lower[:, 0, :], update[:, 0, :], full)
    rest = update[:, 1, :] - dot(couple, first, full)
    second = dot(lower[:, 1, :], rest, full)
    stacked = jnp.concatenate([first, second], axis=0)
    cut = lax.dynamic_slice_in_dim(stacked, rank % fanout * narrow, narrow, 1)
    mine = lax.axis_index("col") == rank // fanout
    picked = lax.psum(jnp.where(mine, cut, jnp.zeros_like(cut)), "col")
    return lax.dot_general(
        picked, stacked, (((0,), (0,)), ((), ())), precision=full, preferred_element_type=jnp.float32
    )


def solution(mesh):
    body = local if (mesh.shape["row"], mesh.shape["col"]) == (8, 4) else local_any
    return jax.shard_map(
        body,
        mesh=mesh,
        in_specs=(
            P(None, None, "row"),
            P("row", "col"),
            P("row", None, "col"),
            P("row", None, None),
            P("row", None),
        ),
        out_specs=P("row", "col"),
        check_vma=False,
    )
```

```python
import functools

import jax
import jax.numpy as jnp
from jax import lax
from jax.experimental import pallas as pl
from jax.experimental.pallas import tpu as pltpu
from jax.sharding import PartitionSpec as P

def dot(a, b, precision=lax.Precision.HIGHEST):
    return jnp.dot(a, b, precision=precision, preferred_element_type=jnp.float32)


def halves(x):
    high = x.astype(jnp.bfloat16)
    return high, (x - high.astype(jnp.float32)).astype(jnp.bfloat16)


def product(a, b, contract=1):
    return lax.dot_general(
        a, b, (((contract,), (0,)), ((), ())), preferred_element_type=jnp.float32
    )


def three(a, b, contract=1):
    (a_high, a_low), (b_high, b_low) = a, b
    small = product(a_high, b_low, contract) + product(a_low, b_high, contract)
    return product(a_high, b_high, contract) + small


def cost(flops, moved):
    return pl.CostEstimate(flops=flops // 32, bytes_accessed=moved // 32, transcendentals=0)


def roomy(limit=62):
    return pltpu.CompilerParams(vmem_limit_bytes=limit << 20)


def corner_kernel(table, *outs):
    depth = table.shape[0] * table.shape[2]
    first, second, couple = [halves(table[:, n].reshape(depth, -1)) for n in range(3)]
    corner = -three(second, halves(three(couple, first)))
    outs[0][...], outs[1][...] = first
    outs[2][...], outs[3][...] = halves(corner)
    outs[4][...], outs[5][...] = second


def transfer_matrix(inverses, coupling):
    table = jnp.concatenate([jnp.swapaxes(inverses, 0, 1), coupling[None]], axis=0)
    table = lax.all_gather(table, "row", axis=0)
    panel = coupling.shape[1]
    return pl.pallas_call(
        corner_kernel,
        out_shape=[jax.ShapeDtypeStruct((panel, panel), jnp.bfloat16)] * 6,
        compiler_params=roomy(),
        cost_estimate=cost(12 * panel**3, 24 * panel**2),
    )(table)


def partial_updates(steps, info, f_own, f_given, p_own, p_given, c_own, c_given, *refs):
    outs, (f_high, f_low) = refs[:-2], refs[-2:]
    step = pl.program_id(0)
    depth, span = f_own.shape
    near = c_own.shape[1]

    @pl.when(step == 0)
    def _():
        for side, part in enumerate((f_own, f_given)):
            cut = slice(side * span, (side + 1) * span)
            f_high[:, cut], f_low[:, cut] = halves(part[...])

    columns = jnp.concatenate([p_own[...], p_given[...]], axis=0)
    total = -three((f_high[...], f_low[...]), halves(columns))
    for n, parts in enumerate(steps):

        @pl.when(step == n)
        def _(parts=parts):
            for out, start, taken, size in parts:
                into, cut = slice(start, start + size), slice(taken, taken + size)
                outs[out][:, into] = total[:, cut]
                for part, rank in ((c_own, info[-2]), (c_given, info[-1])):
                    for k in range(2):
                        rows = pl.ds(pl.multiple_of(k * (depth // 2) + rank * near, near), near)
                        outs[out][rows, into] = outs[out][rows, into] + part[k][:, cut]


def update_blocks(info, steps, widths, sources):
    f_own, _, p_own, _, c_own, _ = sources
    depth, span = f_own.shape
    near = c_own.shape[1]
    wide = p_own.shape[1] // 16
    count = len(steps)
    own = lambda i, info: info[count] * 8 + info[i]
    return pl.pallas_call(
        lambda info, *refs: partial_updates(
            steps, [info[count + n] for n in range(3)], *refs
        ),
        grid_spec=pltpu.PrefetchScalarGridSpec(
            num_scalar_prefetch=1,
            grid=(count,),
            in_specs=[
                pl.BlockSpec((depth, span), lambda i, info: (0, 0)),
                pl.BlockSpec((depth, span), lambda i, info: (0, 0)),
                pl.BlockSpec((span, wide), lambda i, info: (0, own(i, info))),
                pl.BlockSpec((span, wide), lambda i, info: (0, info[i])),
                pl.BlockSpec((2, near, wide), lambda i, info: (0, 0, own(i, info))),
                pl.BlockSpec((2, near, wide), lambda i, info: (0, 0, info[i])),
            ],
            out_specs=[pl.BlockSpec((depth, w), lambda i, info: (0, 0)) for w in widths],
            scratch_shapes=[pltpu.VMEM((depth, 2 * span), jnp.bfloat16)] * 2,
        ),
        out_shape=[jax.ShapeDtypeStruct((depth, w), jnp.float32) for w in widths],
        compiler_params=roomy(),
        cost_estimate=cost(
            6 * depth * 2 * span * count * wide, 4 * depth * (2 * span + count * wide)
        ),
    )(info, *sources)


def solve_kernel(*refs):
    matrix, (keep, a_got, b_got, a_last, b_last) = refs[:6], refs[6:11]
    solved, chunks = refs[11], refs[12:]
    panel, half = keep.shape[0] // 2, a_last.shape[1]
    arrived = [
        got[...] + last[...] for got, last in ((a_got, a_last), (b_got, b_last))
    ]
    update = keep[...] + jnp.concatenate(arrived, axis=1)
    upper, lower = halves(update[:panel]), halves(update[panel:])
    first, corner, second = [(matrix[n][...], matrix[n + 1][...]) for n in (0, 2, 4)]
    top = three(first, upper)
    low = three(corner, upper) + three(second, lower)
    solved[:panel, :] = top
    solved[panel:, :] = low
    for n, chunk in enumerate(chunks):
        cut = slice(n * chunk.shape[1], (n + 1) * chunk.shape[1])
        chunk[:panel, :] = top[:, cut]
        chunk[panel:, :] = low[:, cut]


def solve(matrix, terms, widths, whole):
    panel = matrix[0].shape[0]
    depth, wide = terms[0].shape
    shape = lambda w: jax.ShapeDtypeStruct((depth, w), jnp.float32)
    full = lambda x: pl.BlockSpec(x.shape, lambda i: (0, 0))
    ins = [*matrix, *terms]
    kernel, specs, side, aliases = solve_kernel, [full(x) for x in ins], 0, {}
    if whole is not None:
        kernel = lambda *refs: solve_kernel(*refs[:11], *refs[12:])
        specs, side, aliases = [*specs, pl.BlockSpec(memory_space=pl.ANY)], 1, {11: 0}
        ins = [*ins, whole]
    return pl.pallas_call(
        kernel,
        grid=(1,),
        in_specs=specs,
        out_specs=[pl.BlockSpec((depth, wide), lambda i: (0, side))]
        + [pl.BlockSpec((depth, w), lambda i: (0, 0)) for w in widths],
        out_shape=[shape(2 * wide)] + [shape(w) for w in widths],
        input_output_aliases=aliases,
        compiler_params=roomy(),
        cost_estimate=cost(18 * panel * panel * wide, 4 * (3 * panel**2 + 6 * depth * wide)),
    )(*ins)


def split_kernel(parts, count, place, *refs):
    del place
    high, low = refs[-2:]
    for m in range(count):

        @pl.when(pl.program_id(0) // parts == m)
        def _(block=refs[m]):
            high[0], low[0] = halves(block[...])


def split_blocks(place, blocks, held, weight=1):
    depth, width = blocks[0].shape
    count, parts = len(blocks), 2
    rows = depth // parts
    shape = jax.ShapeDtypeStruct((8, depth, width), jnp.bfloat16)
    spec = pl.BlockSpec((1, rows, width), lambda i, place: (place[i // parts], i % parts, 0))

    def taken(m):
        return pl.BlockSpec(
            (rows, width), lambda i, place: (jnp.clip(i - parts * m, 0, parts - 1), 0)
        )

    held = list(held)
    return pl.pallas_call(
        functools.partial(split_kernel, parts, count),
        grid_spec=pltpu.PrefetchScalarGridSpec(
            num_scalar_prefetch=1,
            grid=(count * parts,),
            in_specs=[taken(m) for m in range(count)]
            + [pl.BlockSpec(memory_space=pl.ANY)] * len(held),
            out_specs=[spec, spec],
        ),
        out_shape=[shape, shape],
        input_output_aliases={count + 1: 0, count + 2: 1} if held else {},
        compiler_params=roomy(),
        cost_estimate=cost(0, 8 * count * depth * width * weight),
    )(place, *blocks, *held)


def downdate_kernel(pieces, high, low, *refs):
    out, left_high, left_low = refs[-3:]
    count, _, width = pieces.shape

    @pl.when(pl.program_id(0) == 0)
    def _():
        for j in range(count):
            cut = slice(j * width, (j + 1) * width)
            left_high[:, cut], left_low[:, cut] = halves(pieces[j])

    total = three((left_high[...], left_low[...]), (high[0], low[0]), 0)
    for j in range(count):
        out[j] = total[j * width : (j + 1) * width]


def downdate_part(pieces, held, out, at):
    count, depth, width = pieces.shape
    wide = held[0].shape[2]
    rows = count * width
    specs = [pl.BlockSpec((count, depth, width), lambda j: (0, 0, 0))]
    specs += [pl.BlockSpec((1, depth, wide), lambda j: (j, 0, 0))] * 2
    ins = [pieces, *held]
    aliases = {}
    if out is not None:
        specs += [pl.BlockSpec(memory_space=pl.ANY)]
        ins += [out]
        aliases = {3: 0}
    return pl.pallas_call(
        downdate_kernel,
        grid=(8,),
        in_specs=specs,
        out_specs=pl.BlockSpec((count, width, wide), lambda j: (0, at, j)),
        out_shape=jax.ShapeDtypeStruct((count, wide, 8 * wide), jnp.float32),
        scratch_shapes=[pltpu.VMEM((depth, rows), jnp.bfloat16)] * 2,
        input_output_aliases=aliases,
        compiler_params=roomy(),
        cost_estimate=cost(
            6 * depth * rows * 8 * wide, 4 * (depth * rows + 8 * depth * wide + rows * 8 * wide)
        ),
    )(*ins)


CORE = [(i, i ^ 1) for i in range(8)]
ALONG_X = [(i, i ^ 2) for i in range(8)]
ALONG_Y = [(i, i ^ 4) for i in range(8)]


SAME_CORE = [[0, 2, 4, 6], [1, 3, 5, 7]]


def to_chips(blocks):
    return lax.all_to_all(blocks, "row", 0, 0, axis_index_groups=SAME_CORE)


def after(x, *others):
    return lax.optimization_barrier((x, *others))[0]


def local(factor_rows, prev_solution, cross_rows, inverses, coupling):
    rank, plane = lax.axis_index("row"), lax.axis_index("col")
    chip, core = rank // 2, rank % 2
    depth = 2 * factor_rows.shape[0]
    width = prev_solution.shape[1]
    half, quarter = width // 16, width // 32
    ints = lambda *values: jnp.stack([jnp.asarray(v, jnp.int32) for v in values])

    matrix = transfer_matrix(inverses, coupling)
    there = lambda x: lax.dynamic_slice_in_dim(
        x, (1 - core) * (width // 2), width // 2, x.ndim - 1
    )
    p_given = lax.ppermute(there(prev_solution), "row", CORE)
    c_own = jnp.swapaxes(cross_rows, 0, 1)
    c_given = lax.ppermute(there(c_own), "row", CORE)
    f_own = jnp.swapaxes(factor_rows, 0, 1).reshape(depth, -1)
    f_given = lax.ppermute(f_own, "row", CORE)
    sources = (f_own, f_given, prev_solution, p_given, c_own, c_given)

    away = (
        ((0, 0, 0, quarter), (1, 0, quarter, quarter)),
        ((2, 0, 0, quarter), (5, 0, quarter, quarter)),
        ((4, 0, 0, quarter), (3, 0, quarter, quarter)),
    )

    def updates(places, steps, widths):
        spots = [(chip ^ across) * 2 + side for across, side in places]
        return update_blocks(ints(*spots, core, rank, rank ^ 1), steps, widths, sources)

    early = updates(((3, 0), (1, 0), (2, 0)), away, (quarter,) * 6)
    *late, keep, late_keep = updates(
        ((3, 1), (1, 1), (2, 1), (0, 0), (0, 1)),
        (*away, ((6, 0, 0, half),), ((7, 0, 0, half),)),
        (*(quarter,) * 6, half, half),
    )

    def passed(a_pass, b_pass):
        return lax.ppermute(a_pass, "row", ALONG_X), lax.ppermute(b_pass, "row", ALONG_Y)

    def arrivals(first, a_send, b_send, a_on, b_on):
        a_got, b_got = passed(a_send, b_send)
        a_last = lax.ppermute(a_on + first[0], "row", ALONG_Y)
        b_last = lax.ppermute(b_on + first[1], "row", ALONG_X)
        return a_got, b_got, a_last, b_last

    first = passed(*early[:2])
    first = after(first[0], late_keep, matrix[0]), first[1]
    terms = arrivals(first, *early[2:])
    first = passed(*[after(x, terms[0]) for x in late[:2]])
    solved, chunk = solve(matrix, (keep, *terms), (half,), None)
    late_terms = arrivals(first, *late[2:])
    solved, *chunks = solve(matrix, (late_keep, *late_terms), (quarter, quarter), solved)
    blocks = [lax.all_gather(x, "col", axis=0) for x in (chunk, *chunks)]

    from_x = lax.ppermute(solved, "row", ALONG_X)
    from_y = lax.ppermute(solved, "row", ALONG_Y)
    twin = lax.ppermute(solved, "row", CORE)

    def split(blocks, pair, group, held, weight=1):
        places = [c * 4 + (chip ^ m) for c in (core, 1 - core) for m in group]
        return split_blocks(ints(*places), [*blocks, *pair], held, weight)

    def given(*arrays):
        return [lax.ppermute(x, "row", CORE) for x in arrays]

    held = split([solved], [twin], (0,), ())
    first_chunk = blocks[0][:, :, :quarter]
    from_x, from_y = after(from_x, first_chunk, *held), after(from_y, first_chunk, *held)
    far_a = lax.ppermute(from_x[:, :half], "row", ALONG_Y)
    far_b = lax.ppermute(from_y[:, half:], "row", ALONG_X)

    held = split([from_x, from_y], given(from_x, from_y), (1, 2), held)
    far = jnp.concatenate([after(far_a, *held), far_b], axis=1)
    pieces = to_chips(first_chunk)
    twin = given(far)
    held = split([after(far, pieces, blocks[1])], twin, (3,), held)
    out = before = downdate_part(pieces, held, None, 0)
    pieces = to_chips(blocks[0][:, :, quarter:])
    out = downdate_part(pieces, held, out, 1)
    pieces = to_chips(after(blocks[1], before))
    before, out = out, downdate_part(pieces, held, out, 2)
    pieces = to_chips(after(blocks[2], before))
    out = downdate_part(pieces, held, out, 3)
    return out.reshape(-1, width)


def local_any(factor_rows, prev_solution, cross_rows, inverses, coupling):
    full = lax.Precision.HIGHEST
    width = prev_solution.shape[1]
    fanout = lax.axis_size("row") // lax.axis_size("col")
    narrow = width // fanout
    rank = lax.axis_index("row")
    sums = lax.psum_scatter(
        jnp.einsum(
            "pks,sn->pkn",
            factor_rows,
            prev_solution,
            precision=full,
            preferred_element_type=jnp.float32,
        ),
        "row",
        scatter_dimension=0,
        tiled=True,
    )
    update = lax.all_gather(cross_rows - sums, "row", axis=0, tiled=True)
    lower = lax.all_gather(inverses, "row", axis=0, tiled=True)
    couple = lax.all_gather(coupling, "row", axis=0, tiled=True)
    first = dot(lower[:, 0, :], update[:, 0, :], full)
    rest = update[:, 1, :] - dot(couple, first, full)
    second = dot(lower[:, 1, :], rest, full)
    stacked = jnp.concatenate([first, second], axis=0)
    cut = lax.dynamic_slice_in_dim(stacked, rank % fanout * narrow, narrow, 1)
    mine = lax.axis_index("col") == rank // fanout
    picked = lax.psum(jnp.where(mine, cut, jnp.zeros_like(cut)), "col")
    return lax.dot_general(
        picked, stacked, (((0,), (0,)), ((), ())), precision=full, preferred_element_type=jnp.float32
    )


def solution(mesh):
    body = local if (mesh.shape["row"], mesh.shape["col"]) == (8, 4) else local_any
    return jax.shard_map(
        body,
        mesh=mesh,
        in_specs=(
            P(None, None, "row"),
            P("row", "col"),
            P("row", None, "col"),
            P("row", None, None),
            P("row", None),
        ),
        out_specs=P("row", "col"),
        check_vma=False,
    )
```

```python
import functools

import jax
import jax.numpy as jnp
from jax import lax
from jax.experimental import pallas as pl
from jax.experimental.pallas import tpu as pltpu
from jax.sharding import PartitionSpec as P

def dot(a, b, precision=lax.Precision.HIGHEST):
    return jnp.dot(a, b, precision=precision, preferred_element_type=jnp.float32)


def halves(x):
    high = x.astype(jnp.bfloat16)
    return high, (x - high.astype(jnp.float32)).astype(jnp.bfloat16)


def product(a, b, contract=1):
    return lax.dot_general(
        a, b, (((contract,), (0,)), ((), ())), preferred_element_type=jnp.float32
    )


def three(a, b, contract=1):
    (a_high, a_low), (b_high, b_low) = a, b
    small = product(a_high, b_low, contract) + product(a_low, b_high, contract)
    return product(a_high, b_high, contract) + small


def cost(flops, moved):
    return pl.CostEstimate(flops=flops // 32, bytes_accessed=moved // 32, transcendentals=0)


def roomy(limit=62):
    return pltpu.CompilerParams(vmem_limit_bytes=limit << 20)


def corner_kernel(table, *outs):
    depth = table.shape[0] * table.shape[2]
    first, second, couple = [halves(table[:, n].reshape(depth, -1)) for n in range(3)]
    corner = -three(second, halves(three(couple, first)))
    outs[0][...], outs[1][...] = first
    outs[2][...], outs[3][...] = halves(corner)
    outs[4][...], outs[5][...] = second


def transfer_matrix(inverses, coupling):
    table = jnp.concatenate([jnp.swapaxes(inverses, 0, 1), coupling[None]], axis=0)
    table = lax.all_gather(table, "row", axis=0)
    panel = coupling.shape[1]
    return pl.pallas_call(
        corner_kernel,
        out_shape=[jax.ShapeDtypeStruct((panel, panel), jnp.bfloat16)] * 6,
        compiler_params=roomy(),
        cost_estimate=cost(12 * panel**3, 24 * panel**2),
    )(table)


def partial_updates(steps, info, f_own, f_given, p_own, p_given, c_own, c_given, *refs):
    outs, (f_high, f_low) = refs[:-2], refs[-2:]
    step = pl.program_id(0)
    depth, span = f_own.shape
    near = c_own.shape[1]

    @pl.when(step == 0)
    def _():
        for side, part in enumerate((f_own, f_given)):
            cut = slice(side * span, (side + 1) * span)
            f_high[:, cut], f_low[:, cut] = halves(part[...])

    columns = jnp.concatenate([p_own[...], p_given[...]], axis=0)
    total = -three((f_high[...], f_low[...]), halves(columns))
    for n, parts in enumerate(steps):

        @pl.when(step == n)
        def _(parts=parts):
            for out, start, taken, size in parts:
                into, cut = slice(start, start + size), slice(taken, taken + size)
                outs[out][:, into] = total[:, cut]
                for part, rank in ((c_own, info[-2]), (c_given, info[-1])):
                    for k in range(2):
                        rows = pl.ds(pl.multiple_of(k * (depth // 2) + rank * near, near), near)
                        outs[out][rows, into] = outs[out][rows, into] + part[k][:, cut]


def update_blocks(info, steps, widths, sources):
    f_own, _, p_own, _, c_own, _ = sources
    depth, span = f_own.shape
    near = c_own.shape[1]
    wide = p_own.shape[1] // 16
    count = len(steps)
    own = lambda i, info: info[count] * 8 + info[i]
    return pl.pallas_call(
        lambda info, *refs: partial_updates(
            steps, [info[count + n] for n in range(3)], *refs
        ),
        grid_spec=pltpu.PrefetchScalarGridSpec(
            num_scalar_prefetch=1,
            grid=(count,),
            in_specs=[
                pl.BlockSpec((depth, span), lambda i, info: (0, 0)),
                pl.BlockSpec((depth, span), lambda i, info: (0, 0)),
                pl.BlockSpec((span, wide), lambda i, info: (0, own(i, info))),
                pl.BlockSpec((span, wide), lambda i, info: (0, info[i])),
                pl.BlockSpec((2, near, wide), lambda i, info: (0, 0, own(i, info))),
                pl.BlockSpec((2, near, wide), lambda i, info: (0, 0, info[i])),
            ],
            out_specs=[pl.BlockSpec((depth, w), lambda i, info: (0, 0)) for w in widths],
            scratch_shapes=[pltpu.VMEM((depth, 2 * span), jnp.bfloat16)] * 2,
        ),
        out_shape=[jax.ShapeDtypeStruct((depth, w), jnp.float32) for w in widths],
        compiler_params=roomy(),
        cost_estimate=cost(
            6 * depth * 2 * span * count * wide, 4 * depth * (2 * span + count * wide)
        ),
    )(info, *sources)


def solve_kernel(*refs):
    matrix, (keep, a_got, b_got, a_last, b_last) = refs[:6], refs[6:11]
    solved, chunks = refs[11], refs[12:]
    panel, half = keep.shape[0] // 2, a_last.shape[1]
    arrived = [
        got[...] + last[...] for got, last in ((a_got, a_last), (b_got, b_last))
    ]
    update = keep[...] + jnp.concatenate(arrived, axis=1)
    upper, lower = halves(update[:panel]), halves(update[panel:])
    first, corner, second = [(matrix[n][...], matrix[n + 1][...]) for n in (0, 2, 4)]
    top = three(first, upper)
    low = three(corner, upper) + three(second, lower)
    solved[:panel, :] = top
    solved[panel:, :] = low
    start = 0
    for chunk in chunks:
        cut = slice(start % (2 * half), start % (2 * half) + chunk.shape[1])
        start = cut.stop
        chunk[:panel, :] = top[:, cut]
        chunk[panel:, :] = low[:, cut]


def solve(matrix, terms, widths, whole):
    panel = matrix[0].shape[0]
    depth, wide = terms[0].shape
    shape = lambda w: jax.ShapeDtypeStruct((depth, w), jnp.float32)
    full = lambda x: pl.BlockSpec(x.shape, lambda i: (0, 0))
    ins = [*matrix, *terms]
    kernel, specs, side, aliases = solve_kernel, [full(x) for x in ins], 0, {}
    if whole is not None:
        kernel = lambda *refs: solve_kernel(*refs[:11], *refs[12:])
        specs, side, aliases = [*specs, pl.BlockSpec(memory_space=pl.ANY)], 1, {11: 0}
        ins = [*ins, whole]
    return pl.pallas_call(
        kernel,
        grid=(1,),
        in_specs=specs,
        out_specs=[pl.BlockSpec((depth, wide), lambda i: (0, side))]
        + [pl.BlockSpec((depth, w), lambda i: (0, 0)) for w in widths],
        out_shape=[shape(2 * wide)] + [shape(w) for w in widths],
        input_output_aliases=aliases,
        compiler_params=roomy(),
        cost_estimate=cost(18 * panel * panel * wide, 4 * (3 * panel**2 + 6 * depth * wide)),
    )(*ins)


def split_kernel(parts, count, place, *refs):
    del place
    high, low = refs[-2:]
    for m in range(count):

        @pl.when(pl.program_id(0) // parts == m)
        def _(block=refs[m]):
            high[0], low[0] = halves(block[...])


def split_blocks(place, blocks, held):
    depth, width = blocks[0].shape
    count, parts = len(blocks), 2
    rows = depth // parts
    held = list(held)
    wide = held[0].shape[2] if held else width
    shape = jax.ShapeDtypeStruct((8, depth, wide), jnp.bfloat16)
    spec = pl.BlockSpec(
        (1, rows, width), lambda i, place: (place[0, i // parts], i % parts, place[1, i // parts])
    )

    def taken(m):
        return pl.BlockSpec(
            (rows, width), lambda i, place: (jnp.clip(i - parts * m, 0, parts - 1), 0)
        )

    return pl.pallas_call(
        functools.partial(split_kernel, parts, count),
        grid_spec=pltpu.PrefetchScalarGridSpec(
            num_scalar_prefetch=1,
            grid=(count * parts,),
            in_specs=[taken(m) for m in range(count)]
            + [pl.BlockSpec(memory_space=pl.ANY)] * len(held),
            out_specs=[spec, spec],
        ),
        out_shape=[shape, shape],
        input_output_aliases={count + 1: 0, count + 2: 1} if held else {},
        compiler_params=roomy(),
        cost_estimate=cost(0, 8 * count * depth * width),
    )(place, *blocks, *held)


def downdate_kernel(pieces, high, low, *refs):
    out, left_high, left_low = refs[-3:]
    count, _, width = pieces.shape

    @pl.when(pl.program_id(0) == 0)
    def _():
        for j in range(count):
            cut = slice(j * width, (j + 1) * width)
            left_high[:, cut], left_low[:, cut] = halves(pieces[j])

    total = three((left_high[...], left_low[...]), (high[0], low[0]), 0)
    for j in range(count):
        out[j] = total[j * width : (j + 1) * width]


def downdate_part(pieces, held, out, at):
    count, depth, width = pieces.shape
    wide = held[0].shape[2]
    rows = count * width
    specs = [pl.BlockSpec((count, depth, width), lambda j: (0, 0, 0))]
    specs += [pl.BlockSpec((1, depth, wide), lambda j: (j, 0, 0))] * 2
    ins = [pieces, *held]
    aliases = {}
    if out is not None:
        specs += [pl.BlockSpec(memory_space=pl.ANY)]
        ins += [out]
        aliases = {3: 0}
    return pl.pallas_call(
        downdate_kernel,
        grid=(8,),
        in_specs=specs,
        out_specs=pl.BlockSpec((count, width, wide), lambda j: (0, at, j)),
        out_shape=jax.ShapeDtypeStruct((count, wide, 8 * wide), jnp.float32),
        scratch_shapes=[pltpu.VMEM((depth, rows), jnp.bfloat16)] * 2,
        input_output_aliases=aliases,
        compiler_params=roomy(),
        cost_estimate=cost(
            6 * depth * rows * 8 * wide, 4 * (depth * rows + 8 * depth * wide + rows * 8 * wide)
        ),
    )(*ins)


CORE = [(i, i ^ 1) for i in range(8)]
ALONG_X = [(i, i ^ 2) for i in range(8)]
ALONG_Y = [(i, i ^ 4) for i in range(8)]


SAME_CORE = [[0, 2, 4, 6], [1, 3, 5, 7]]


def to_chips(blocks):
    return lax.all_to_all(blocks, "row", 0, 0, axis_index_groups=SAME_CORE)


def after(x, *others):
    return lax.optimization_barrier((x, *others))[0]


def local(factor_rows, prev_solution, cross_rows, inverses, coupling):
    rank, plane = lax.axis_index("row"), lax.axis_index("col")
    chip, core = rank // 2, rank % 2
    depth = 2 * factor_rows.shape[0]
    width = prev_solution.shape[1]
    half, quarter = width // 16, width // 32
    ints = lambda *values: jnp.stack([jnp.asarray(v, jnp.int32) for v in values])

    matrix = transfer_matrix(inverses, coupling)
    there = lambda x: lax.dynamic_slice_in_dim(
        x, (1 - core) * (width // 2), width // 2, x.ndim - 1
    )
    p_given = lax.ppermute(there(prev_solution), "row", CORE)
    c_own = jnp.swapaxes(cross_rows, 0, 1)
    c_given = lax.ppermute(there(c_own), "row", CORE)
    f_own = jnp.swapaxes(factor_rows, 0, 1).reshape(depth, -1)
    f_given = lax.ppermute(f_own, "row", CORE)
    sources = (f_own, f_given, prev_solution, p_given, c_own, c_given)

    away = (
        ((0, 0, 0, quarter), (1, 0, quarter, quarter)),
        ((2, 0, 0, quarter), (5, 0, quarter, quarter)),
        ((4, 0, 0, quarter), (3, 0, quarter, quarter)),
    )

    def updates(places, steps, widths):
        spots = [(chip ^ across) * 2 + side for across, side in places]
        return update_blocks(ints(*spots, core, rank, rank ^ 1), steps, widths, sources)

    shifted = tuple(tuple((out - 2, *rest) for out, *rest in step) for step in away[1:])
    early = updates(((3, 0),), away[:1], (quarter,) * 2)
    early += updates(((1, 0), (2, 0)), shifted, (quarter,) * 4)
    *late, keep, late_keep = updates(
        ((3, 1), (1, 1), (2, 1), (0, 0), (0, 1)),
        (*away, ((6, 0, 0, half),), ((7, 0, 0, half),)),
        (*(quarter,) * 6, half, half),
    )

    def passed(a_pass, b_pass):
        return lax.ppermute(a_pass, "row", ALONG_X), lax.ppermute(b_pass, "row", ALONG_Y)

    def arrivals(first, a_send, b_send, a_on, b_on):
        a_got, b_got = passed(a_send, b_send)
        a_last = lax.ppermute(a_on + first[0], "row", ALONG_Y)
        b_last = lax.ppermute(b_on + first[1], "row", ALONG_X)
        return a_got, b_got, a_last, b_last

    first = passed(*early[:2])
    first = after(first[0], late_keep), first[1]
    terms = arrivals(first, *early[2:])
    first = passed(*[after(x, terms[0]) for x in late[:2]])
    solved, chunk = solve(matrix, (keep, *terms), (half,), None)
    late_terms = arrivals(first, *late[2:])
    solved, late_half, *chunks = solve(
        matrix, (late_keep, *late_terms), (half, quarter, quarter), solved
    )
    blocks = [lax.all_gather(x, "col", axis=0) for x in (chunk, *chunks)]

    x_early = lax.ppermute(after(chunk, late_half), "row", ALONG_X)
    y_late = lax.ppermute(late_half, "row", ALONG_Y)
    x_late = lax.ppermute(late_half, "row", ALONG_X)
    y_early = lax.ppermute(after(chunk, late_half), "row", ALONG_Y)
    twin = lax.ppermute(solved, "row", CORE)

    def split(blocks, pair, spots, held):
        places = [c * 4 + (chip ^ m) for c in (core, 1 - core) for m, _ in spots]
        sides = [side for _, side in spots] * 2
        return split_blocks(jnp.stack([ints(*places), ints(*sides)]), [*blocks, *pair], held)

    def given(*arrays):
        return [lax.ppermute(x, "row", CORE) for x in arrays]

    held = split([solved], [twin], ((0, 0),), ())
    first_chunk = blocks[0][:, :, :quarter]
    x_early, y_late = after(x_early, first_chunk, *held), after(y_late, first_chunk, *held)
    far_a = lax.ppermute(x_early, "row", ALONG_Y)
    far_b = lax.ppermute(y_late, "row", ALONG_X)
    sides = [x_early, x_late, y_early, y_late]
    held = split(sides, given(*sides), ((1, 0), (1, 1), (2, 0), (2, 1)), held)
    far = jnp.concatenate([after(far_a, *held), far_b], axis=1)
    pieces = to_chips(first_chunk)
    twin = given(far)
    held = split([after(far, pieces, blocks[1])], twin, ((3, 0),), held)
    out = before = downdate_part(pieces, held, None, 0)
    pieces = to_chips(blocks[0][:, :, quarter:])
    out = downdate_part(pieces, held, out, 1)
    pieces = to_chips(after(blocks[1], before))
    before, out = out, downdate_part(pieces, held, out, 2)
    pieces = to_chips(after(blocks[2], before))
    out = downdate_part(pieces, held, out, 3)
    return out.reshape(-1, width)


def local_any(factor_rows, prev_solution, cross_rows, inverses, coupling):
    full = lax.Precision.HIGHEST
    width = prev_solution.shape[1]
    fanout = lax.axis_size("row") // lax.axis_size("col")
    narrow = width // fanout
    rank = lax.axis_index("row")
    sums = lax.psum_scatter(
        jnp.einsum(
            "pks,sn->pkn",
            factor_rows,
            prev_solution,
            precision=full,
            preferred_element_type=jnp.float32,
        ),
        "row",
        scatter_dimension=0,
        tiled=True,
    )
    update = lax.all_gather(cross_rows - sums, "row", axis=0, tiled=True)
    lower = lax.all_gather(inverses, "row", axis=0, tiled=True)
    couple = lax.all_gather(coupling, "row", axis=0, tiled=True)
    first = dot(lower[:, 0, :], update[:, 0, :], full)
    rest = update[:, 1, :] - dot(couple, first, full)
    second = dot(lower[:, 1, :], rest, full)
    stacked = jnp.concatenate([first, second], axis=0)
    cut = lax.dynamic_slice_in_dim(stacked, rank % fanout * narrow, narrow, 1)
    mine = lax.axis_index("col") == rank // fanout
    picked = lax.psum(jnp.where(mine, cut, jnp.zeros_like(cut)), "col")
    return lax.dot_general(
        picked, stacked, (((0,), (0,)), ((), ())), precision=full, preferred_element_type=jnp.float32
    )


def solution(mesh):
    body = local if (mesh.shape["row"], mesh.shape["col"]) == (8, 4) else local_any
    return jax.shard_map(
        body,
        mesh=mesh,
        in_specs=(
            P(None, None, "row"),
            P("row", "col"),
            P("row", None, "col"),
            P("row", None, None),
            P("row", None),
        ),
        out_specs=P("row", "col"),
        check_vma=False,
    )
```

```python
import functools

import jax
import jax.numpy as jnp
from jax import lax
from jax.experimental import pallas as pl
from jax.experimental.pallas import tpu as pltpu
from jax.sharding import PartitionSpec as P

def dot(a, b, precision=lax.Precision.HIGHEST):
    return jnp.dot(a, b, precision=precision, preferred_element_type=jnp.float32)


def halves(x):
    high = x.astype(jnp.bfloat16)
    return high, (x - high.astype(jnp.float32)).astype(jnp.bfloat16)


def product(a, b, contract=1):
    return lax.dot_general(
        a, b, (((contract,), (0,)), ((), ())), preferred_element_type=jnp.float32
    )


def three(a, b, contract=1):
    (a_high, a_low), (b_high, b_low) = a, b
    small = product(a_high, b_low, contract) + product(a_low, b_high, contract)
    return product(a_high, b_high, contract) + small


def cost(flops, moved):
    return pl.CostEstimate(flops=flops // 32, bytes_accessed=moved // 32, transcendentals=0)


def roomy(limit=62):
    return pltpu.CompilerParams(vmem_limit_bytes=limit << 20)


def corner_kernel(table, *outs):
    depth = table.shape[0] * table.shape[2]
    first, second, couple = [halves(table[:, n].reshape(depth, -1)) for n in range(3)]
    corner = -three(second, halves(three(couple, first)))
    outs[0][...], outs[1][...] = first
    outs[2][...], outs[3][...] = halves(corner)
    outs[4][...], outs[5][...] = second


def transfer_matrix(inverses, coupling):
    table = jnp.concatenate([jnp.swapaxes(inverses, 0, 1), coupling[None]], axis=0)
    table = lax.all_gather(table, "row", axis=0)
    panel = coupling.shape[1]
    return pl.pallas_call(
        corner_kernel,
        out_shape=[jax.ShapeDtypeStruct((panel, panel), jnp.bfloat16)] * 6,
        compiler_params=roomy(),
        cost_estimate=cost(12 * panel**3, 24 * panel**2),
    )(table)


def partial_updates(steps, info, f_own, f_given, p_own, p_given, c_own, c_given, *refs):
    outs, (f_high, f_low) = refs[:-2], refs[-2:]
    step = pl.program_id(0)
    depth, span = f_own.shape
    near = c_own.shape[1]

    @pl.when(step == 0)
    def _():
        for side, part in enumerate((f_own, f_given)):
            cut = slice(side * span, (side + 1) * span)
            f_high[:, cut], f_low[:, cut] = halves(part[...])

    columns = jnp.concatenate([p_own[...], p_given[...]], axis=0)
    total = -three((f_high[...], f_low[...]), halves(columns))
    for n, parts in enumerate(steps):

        @pl.when(step == n)
        def _(parts=parts):
            for out, start, taken, size in parts:
                into, cut = slice(start, start + size), slice(taken, taken + size)
                outs[out][:, into] = total[:, cut]
                for part, rank in ((c_own, info[-2]), (c_given, info[-1])):
                    for k in range(2):
                        rows = pl.ds(pl.multiple_of(k * (depth // 2) + rank * near, near), near)
                        outs[out][rows, into] = outs[out][rows, into] + part[k][:, cut]


def update_blocks(info, steps, widths, sources):
    f_own, _, p_own, _, c_own, _ = sources
    depth, span = f_own.shape
    near = c_own.shape[1]
    wide = p_own.shape[1] // 16
    count = len(steps)
    own = lambda i, info: info[count] * 8 + info[i]
    return pl.pallas_call(
        lambda info, *refs: partial_updates(
            steps, [info[count + n] for n in range(3)], *refs
        ),
        grid_spec=pltpu.PrefetchScalarGridSpec(
            num_scalar_prefetch=1,
            grid=(count,),
            in_specs=[
                pl.BlockSpec((depth, span), lambda i, info: (0, 0)),
                pl.BlockSpec((depth, span), lambda i, info: (0, 0)),
                pl.BlockSpec((span, wide), lambda i, info: (0, own(i, info))),
                pl.BlockSpec((span, wide), lambda i, info: (0, info[i])),
                pl.BlockSpec((2, near, wide), lambda i, info: (0, 0, own(i, info))),
                pl.BlockSpec((2, near, wide), lambda i, info: (0, 0, info[i])),
            ],
            out_specs=[pl.BlockSpec((depth, w), lambda i, info: (0, 0)) for w in widths],
            scratch_shapes=[pltpu.VMEM((depth, 2 * span), jnp.bfloat16)] * 2,
        ),
        out_shape=[jax.ShapeDtypeStruct((depth, w), jnp.float32) for w in widths],
        compiler_params=roomy(),
        cost_estimate=cost(
            6 * depth * 2 * span * count * wide, 4 * depth * (2 * span + count * wide)
        ),
    )(info, *sources)


def solve_kernel(*refs):
    matrix, (keep, a_got, b_got, a_last, b_last) = refs[:6], refs[6:11]
    solved, chunks = refs[11], refs[12:]
    panel, half = keep.shape[0] // 2, a_last.shape[1]
    arrived = [
        got[...] + last[...] for got, last in ((a_got, a_last), (b_got, b_last))
    ]
    update = keep[...] + jnp.concatenate(arrived, axis=1)
    upper, lower = halves(update[:panel]), halves(update[panel:])
    first, corner, second = [(matrix[n][...], matrix[n + 1][...]) for n in (0, 2, 4)]
    top = three(first, upper)
    low = three(corner, upper) + three(second, lower)
    solved[:panel, :] = top
    solved[panel:, :] = low
    start = 0
    for chunk in chunks:
        cut = slice(start % (2 * half), start % (2 * half) + chunk.shape[1])
        start = cut.stop
        chunk[:panel, :] = top[:, cut]
        chunk[panel:, :] = low[:, cut]


def solve(matrix, terms, widths, whole):
    panel = matrix[0].shape[0]
    depth, wide = terms[0].shape
    shape = lambda w: jax.ShapeDtypeStruct((depth, w), jnp.float32)
    full = lambda x: pl.BlockSpec(x.shape, lambda i: (0, 0))
    ins = [*matrix, *terms]
    kernel, specs, side, aliases = solve_kernel, [full(x) for x in ins], 0, {}
    if whole is not None:
        kernel = lambda *refs: solve_kernel(*refs[:11], *refs[12:])
        specs, side, aliases = [*specs, pl.BlockSpec(memory_space=pl.ANY)], 1, {11: 0}
        ins = [*ins, whole]
    return pl.pallas_call(
        kernel,
        grid=(1,),
        in_specs=specs,
        out_specs=[pl.BlockSpec((depth, wide), lambda i: (0, side))]
        + [pl.BlockSpec((depth, w), lambda i: (0, 0)) for w in widths],
        out_shape=[shape(2 * wide)] + [shape(w) for w in widths],
        input_output_aliases=aliases,
        compiler_params=roomy(),
        cost_estimate=cost(18 * panel * panel * wide, 4 * (3 * panel**2 + 6 * depth * wide)),
    )(*ins)


def split_kernel(parts, count, place, *refs):
    del place
    high, low = refs[-2:]
    for m in range(count):

        @pl.when(pl.program_id(0) // parts == m)
        def _(block=refs[m]):
            high[0], low[0] = halves(block[...])


def split_blocks(place, blocks, held):
    depth, width = blocks[0].shape
    count, parts = len(blocks), 2
    rows = depth // parts
    held = list(held)
    wide = held[0].shape[2] if held else width
    shape = jax.ShapeDtypeStruct((8, depth, wide), jnp.bfloat16)
    spec = pl.BlockSpec(
        (1, rows, width), lambda i, place: (place[0, i // parts], i % parts, place[1, i // parts])
    )

    def taken(m):
        return pl.BlockSpec(
            (rows, width), lambda i, place: (jnp.clip(i - parts * m, 0, parts - 1), 0)
        )

    return pl.pallas_call(
        functools.partial(split_kernel, parts, count),
        grid_spec=pltpu.PrefetchScalarGridSpec(
            num_scalar_prefetch=1,
            grid=(count * parts,),
            in_specs=[taken(m) for m in range(count)]
            + [pl.BlockSpec(memory_space=pl.ANY)] * len(held),
            out_specs=[spec, spec],
        ),
        out_shape=[shape, shape],
        input_output_aliases={count + 1: 0, count + 2: 1} if held else {},
        compiler_params=roomy(),
        cost_estimate=cost(0, 8 * count * depth * width),
    )(place, *blocks, *held)


def downdate_kernel(pieces, high, low, *refs):
    out, left_high, left_low = refs[-3:]
    count, _, width = pieces.shape

    @pl.when(pl.program_id(0) == 0)
    def _():
        for j in range(count):
            cut = slice(j * width, (j + 1) * width)
            left_high[:, cut], left_low[:, cut] = halves(pieces[j])

    total = three((left_high[...], left_low[...]), (high[0], low[0]), 0)
    for j in range(count):
        out[j] = total[j * width : (j + 1) * width]


def downdate_part(pieces, held, out, at):
    count, depth, width = pieces.shape
    wide = held[0].shape[2]
    rows = count * width
    specs = [pl.BlockSpec((count, depth, width), lambda j: (0, 0, 0))]
    specs += [pl.BlockSpec((1, depth, wide), lambda j: (j, 0, 0))] * 2
    ins = [pieces, *held]
    aliases = {}
    if out is not None:
        specs += [pl.BlockSpec(memory_space=pl.ANY)]
        ins += [out]
        aliases = {3: 0}
    return pl.pallas_call(
        downdate_kernel,
        grid=(8,),
        in_specs=specs,
        out_specs=pl.BlockSpec((count, width, wide), lambda j: (0, at, j)),
        out_shape=jax.ShapeDtypeStruct((count, wide, 8 * wide), jnp.float32),
        scratch_shapes=[pltpu.VMEM((depth, rows), jnp.bfloat16)] * 2,
        input_output_aliases=aliases,
        compiler_params=roomy(),
        cost_estimate=cost(
            6 * depth * rows * 8 * wide, 4 * (depth * rows + 8 * depth * wide + rows * 8 * wide)
        ),
    )(*ins)


CORE = [(i, i ^ 1) for i in range(8)]
ALONG_X = [(i, i ^ 2) for i in range(8)]
ALONG_Y = [(i, i ^ 4) for i in range(8)]


SAME_CORE = [[0, 2, 4, 6], [1, 3, 5, 7]]


def to_chips(blocks):
    return lax.all_to_all(blocks, "row", 0, 0, axis_index_groups=SAME_CORE)


def after(x, *others):
    return lax.optimization_barrier((x, *others))[0]


def local(factor_rows, prev_solution, cross_rows, inverses, coupling):
    rank, plane = lax.axis_index("row"), lax.axis_index("col")
    chip, core = rank // 2, rank % 2
    depth = 2 * factor_rows.shape[0]
    width = prev_solution.shape[1]
    half, quarter = width // 16, width // 32
    ints = lambda *values: jnp.stack([jnp.asarray(v, jnp.int32) for v in values])

    matrix = transfer_matrix(inverses, coupling)
    there = lambda x: lax.dynamic_slice_in_dim(
        x, (1 - core) * (width // 2), width // 2, x.ndim - 1
    )
    p_given = lax.ppermute(there(prev_solution), "row", CORE)
    c_own = jnp.swapaxes(cross_rows, 0, 1)
    c_given = lax.ppermute(there(c_own), "row", CORE)
    f_own = jnp.swapaxes(factor_rows, 0, 1).reshape(depth, -1)
    f_given = lax.ppermute(f_own, "row", CORE)
    sources = (f_own, f_given, prev_solution, p_given, c_own, c_given)

    away = (
        ((0, 0, 0, quarter), (1, 0, quarter, quarter)),
        ((2, 0, 0, quarter), (5, 0, quarter, quarter)),
        ((4, 0, 0, quarter), (3, 0, quarter, quarter)),
    )

    def updates(places, steps, widths):
        spots = [(chip ^ across) * 2 + side for across, side in places]
        return update_blocks(ints(*spots, core, rank, rank ^ 1), steps, widths, sources)

    shifted = tuple(tuple((out - 2, *rest) for out, *rest in step) for step in away[1:])
    early = updates(((3, 0),), away[:1], (quarter,) * 2)
    early += updates(((1, 0), (2, 0)), shifted, (quarter,) * 4)
    *late, keep, late_keep = updates(
        ((3, 1), (1, 1), (2, 1), (0, 0), (0, 1)),
        (*away, ((6, 0, 0, half),), ((7, 0, 0, half),)),
        (*(quarter,) * 6, half, half),
    )

    def passed(a_pass, b_pass):
        return lax.ppermute(a_pass, "row", ALONG_X), lax.ppermute(b_pass, "row", ALONG_Y)

    def arrivals(first, a_send, b_send, a_on, b_on):
        a_got, b_got = passed(a_send, b_send)
        a_last = lax.ppermute(a_on + first[0], "row", ALONG_Y)
        b_last = lax.ppermute(b_on + first[1], "row", ALONG_X)
        return a_got, b_got, a_last, b_last

    first = passed(*early[:2])
    first = after(first[0], late_keep), first[1]
    terms = arrivals(first, *early[2:])
    first = passed(*[after(x, terms[0]) for x in late[:2]])
    solved, chunk = solve(matrix, (keep, *terms), (half,), None)
    late_terms = arrivals(first, *late[2:])
    solved, late_half, *chunks = solve(
        matrix, (late_keep, *late_terms), (half, quarter, quarter), solved
    )
    blocks = [lax.all_gather(x, "col", axis=0) for x in (after(chunk, *first), *chunks)]

    x_early = lax.ppermute(after(chunk, late_half), "row", ALONG_X)
    y_late = lax.ppermute(late_half, "row", ALONG_Y)
    x_late = lax.ppermute(late_half, "row", ALONG_X)
    y_early = lax.ppermute(after(chunk, late_half), "row", ALONG_Y)
    twin = lax.ppermute(solved, "row", CORE)

    def split(blocks, pair, spots, held):
        places = [c * 4 + (chip ^ m) for c in (core, 1 - core) for m, _ in spots]
        sides = [side for _, side in spots] * 2
        return split_blocks(jnp.stack([ints(*places), ints(*sides)]), [*blocks, *pair], held)

    def given(*arrays):
        return [lax.ppermute(x, "row", CORE) for x in arrays]

    held = split([solved], [twin], ((0, 0),), ())
    first_chunk = blocks[0][:, :, :quarter]
    x_early, y_late = after(x_early, *held), after(y_late, *held)
    x_late, y_early = after(x_late, first_chunk), after(y_early, first_chunk)
    far_a = lax.ppermute(x_early, "row", ALONG_Y)
    far_b = lax.ppermute(y_late, "row", ALONG_X)
    sides = [x_early, x_late, y_early, y_late]
    held = split(sides, given(*sides), ((1, 0), (1, 1), (2, 0), (2, 1)), held)
    second_chunk = after(blocks[0], *held)[:, :, quarter:]
    far = jnp.concatenate([after(far_a, *held), far_b], axis=1)
    pieces = to_chips(first_chunk)
    twin = given(far)
    held = split([after(far, pieces, blocks[1])], twin, ((3, 0),), held)
    out = before = downdate_part(pieces, held, None, 0)
    pieces = to_chips(second_chunk)
    out = downdate_part(pieces, held, out, 1)
    pieces = to_chips(after(blocks[1], before))
    before, out = out, downdate_part(pieces, held, out, 2)
    pieces = to_chips(after(blocks[2], before))
    out = downdate_part(pieces, held, out, 3)
    return out.reshape(-1, width)


def local_any(factor_rows, prev_solution, cross_rows, inverses, coupling):
    full = lax.Precision.HIGHEST
    width = prev_solution.shape[1]
    fanout = lax.axis_size("row") // lax.axis_size("col")
    narrow = width // fanout
    rank = lax.axis_index("row")
    sums = lax.psum_scatter(
        jnp.einsum(
            "pks,sn->pkn",
            factor_rows,
            prev_solution,
            precision=full,
            preferred_element_type=jnp.float32,
        ),
        "row",
        scatter_dimension=0,
        tiled=True,
    )
    update = lax.all_gather(cross_rows - sums, "row", axis=0, tiled=True)
    lower = lax.all_gather(inverses, "row", axis=0, tiled=True)
    couple = lax.all_gather(coupling, "row", axis=0, tiled=True)
    first = dot(lower[:, 0, :], update[:, 0, :], full)
    rest = update[:, 1, :] - dot(couple, first, full)
    second = dot(lower[:, 1, :], rest, full)
    stacked = jnp.concatenate([first, second], axis=0)
    cut = lax.dynamic_slice_in_dim(stacked, rank % fanout * narrow, narrow, 1)
    mine = lax.axis_index("col") == rank // fanout
    picked = lax.psum(jnp.where(mine, cut, jnp.zeros_like(cut)), "col")
    return lax.dot_general(
        picked, stacked, (((0,), (0,)), ((), ())), precision=full, preferred_element_type=jnp.float32
    )


def solution(mesh):
    body = local if (mesh.shape["row"], mesh.shape["col"]) == (8, 4) else local_any
    return jax.shard_map(
        body,
        mesh=mesh,
        in_specs=(
            P(None, None, "row"),
            P("row", "col"),
            P("row", None, "col"),
            P("row", None, None),
            P("row", None),
        ),
        out_specs=P("row", "col"),
        check_vma=False,
    )
```

```python
import functools

import jax
import jax.numpy as jnp
from jax import lax
from jax.experimental import pallas as pl
from jax.experimental.pallas import tpu as pltpu
from jax.sharding import PartitionSpec as P

def dot(a, b, precision=lax.Precision.HIGHEST):
    return jnp.dot(a, b, precision=precision, preferred_element_type=jnp.float32)


def halves(x):
    high = x.astype(jnp.bfloat16)
    return high, (x - high.astype(jnp.float32)).astype(jnp.bfloat16)


def product(a, b, contract=1):
    return lax.dot_general(
        a, b, (((contract,), (0,)), ((), ())), preferred_element_type=jnp.float32
    )


def three(a, b, contract=1):
    (a_high, a_low), (b_high, b_low) = a, b
    small = product(a_high, b_low, contract) + product(a_low, b_high, contract)
    return product(a_high, b_high, contract) + small


def cost(flops, moved):
    return pl.CostEstimate(flops=flops // 32, bytes_accessed=moved // 32, transcendentals=0)


def roomy(limit=62):
    return pltpu.CompilerParams(vmem_limit_bytes=limit << 20)


def corner_kernel(table, *outs):
    depth = table.shape[0] * table.shape[2]
    first, second, couple = [halves(table[:, n].reshape(depth, -1)) for n in range(3)]
    corner = -three(second, halves(three(couple, first)))
    outs[0][...], outs[1][...] = first
    outs[2][...], outs[3][...] = halves(corner)
    outs[4][...], outs[5][...] = second


def transfer_matrix(inverses, coupling):
    table = jnp.concatenate([jnp.swapaxes(inverses, 0, 1), coupling[None]], axis=0)
    table = lax.all_gather(table, "row", axis=0)
    panel = coupling.shape[1]
    return pl.pallas_call(
        corner_kernel,
        out_shape=[jax.ShapeDtypeStruct((panel, panel), jnp.bfloat16)] * 6,
        compiler_params=roomy(),
        cost_estimate=cost(12 * panel**3, 24 * panel**2),
    )(table)


def partial_updates(steps, info, f_own, f_given, p_own, p_given, c_own, c_given, *refs):
    outs, (f_high, f_low) = refs[:-2], refs[-2:]
    step = pl.program_id(0)
    depth, span = f_own.shape
    near = c_own.shape[1]

    @pl.when(step == 0)
    def _():
        for side, part in enumerate((f_own, f_given)):
            cut = slice(side * span, (side + 1) * span)
            f_high[:, cut], f_low[:, cut] = halves(part[...])

    columns = jnp.concatenate([p_own[...], p_given[...]], axis=0)
    total = -three((f_high[...], f_low[...]), halves(columns))
    for n, parts in enumerate(steps):

        @pl.when(step == n)
        def _(parts=parts):
            for out, start, taken, size in parts:
                into, cut = slice(start, start + size), slice(taken, taken + size)
                outs[out][:, into] = total[:, cut]
                for part, rank in ((c_own, info[-2]), (c_given, info[-1])):
                    for k in range(2):
                        rows = pl.ds(pl.multiple_of(k * (depth // 2) + rank * near, near), near)
                        outs[out][rows, into] = outs[out][rows, into] + part[k][:, cut]


def update_blocks(info, steps, widths, sources):
    f_own, _, p_own, _, c_own, _ = sources
    depth, span = f_own.shape
    near = c_own.shape[1]
    wide = p_own.shape[1] // 16
    count = len(steps)
    own = lambda i, info: info[count] * 8 + info[i]
    return pl.pallas_call(
        lambda info, *refs: partial_updates(
            steps, [info[count + n] for n in range(3)], *refs
        ),
        grid_spec=pltpu.PrefetchScalarGridSpec(
            num_scalar_prefetch=1,
            grid=(count,),
            in_specs=[
                pl.BlockSpec((depth, span), lambda i, info: (0, 0)),
                pl.BlockSpec((depth, span), lambda i, info: (0, 0)),
                pl.BlockSpec((span, wide), lambda i, info: (0, own(i, info))),
                pl.BlockSpec((span, wide), lambda i, info: (0, info[i])),
                pl.BlockSpec((2, near, wide), lambda i, info: (0, 0, own(i, info))),
                pl.BlockSpec((2, near, wide), lambda i, info: (0, 0, info[i])),
            ],
            out_specs=[pl.BlockSpec((depth, w), lambda i, info: (0, 0)) for w in widths],
            scratch_shapes=[pltpu.VMEM((depth, 2 * span), jnp.bfloat16)] * 2,
        ),
        out_shape=[jax.ShapeDtypeStruct((depth, w), jnp.float32) for w in widths],
        compiler_params=roomy(),
        cost_estimate=cost(
            6 * depth * 2 * span * count * wide, 4 * depth * (2 * span + count * wide)
        ),
    )(info, *sources)


def solve_kernel(*refs):
    matrix, (keep, a_got, b_got, a_last, b_last) = refs[:6], refs[6:11]
    solved, chunks = refs[11], refs[12:]
    panel, half = keep.shape[0] // 2, a_last.shape[1]
    arrived = [
        got[...] + last[...] for got, last in ((a_got, a_last), (b_got, b_last))
    ]
    update = keep[...] + jnp.concatenate(arrived, axis=1)
    upper, lower = halves(update[:panel]), halves(update[panel:])
    first, corner, second = [(matrix[n][...], matrix[n + 1][...]) for n in (0, 2, 4)]
    top = three(first, upper)
    low = three(corner, upper) + three(second, lower)
    solved[:panel, :] = top
    solved[panel:, :] = low
    start = 0
    for chunk in chunks:
        cut = slice(start % (2 * half), start % (2 * half) + chunk.shape[1])
        start = cut.stop
        chunk[:panel, :] = top[:, cut]
        chunk[panel:, :] = low[:, cut]


def solve(matrix, terms, widths, whole):
    panel = matrix[0].shape[0]
    depth, wide = terms[0].shape
    shape = lambda w: jax.ShapeDtypeStruct((depth, w), jnp.float32)
    full = lambda x: pl.BlockSpec(x.shape, lambda i: (0, 0))
    ins = [*matrix, *terms]
    kernel, specs, side, aliases = solve_kernel, [full(x) for x in ins], 0, {}
    if whole is not None:
        kernel = lambda *refs: solve_kernel(*refs[:11], *refs[12:])
        specs, side, aliases = [*specs, pl.BlockSpec(memory_space=pl.ANY)], 1, {11: 0}
        ins = [*ins, whole]
    return pl.pallas_call(
        kernel,
        grid=(1,),
        in_specs=specs,
        out_specs=[pl.BlockSpec((depth, wide), lambda i: (0, side))]
        + [pl.BlockSpec((depth, w), lambda i: (0, 0)) for w in widths],
        out_shape=[shape(2 * wide)] + [shape(w) for w in widths],
        input_output_aliases=aliases,
        compiler_params=roomy(),
        cost_estimate=cost(18 * panel * panel * wide, 4 * (3 * panel**2 + 6 * depth * wide)),
    )(*ins)


def split_kernel(parts, count, place, *refs):
    del place
    high, low = refs[-2:]
    for m in range(count):

        @pl.when(pl.program_id(0) // parts == m)
        def _(block=refs[m]):
            high[0], low[0] = halves(block[...])


def split_blocks(place, blocks, held):
    depth, width = blocks[0].shape
    count, parts = len(blocks), 2
    rows = depth // parts
    held = list(held)
    wide = held[0].shape[2] if held else width
    shape = jax.ShapeDtypeStruct((8, depth, wide), jnp.bfloat16)
    spec = pl.BlockSpec(
        (1, rows, width), lambda i, place: (place[0, i // parts], i % parts, place[1, i // parts])
    )

    def taken(m):
        return pl.BlockSpec(
            (rows, width), lambda i, place: (jnp.clip(i - parts * m, 0, parts - 1), 0)
        )

    return pl.pallas_call(
        functools.partial(split_kernel, parts, count),
        grid_spec=pltpu.PrefetchScalarGridSpec(
            num_scalar_prefetch=1,
            grid=(count * parts,),
            in_specs=[taken(m) for m in range(count)]
            + [pl.BlockSpec(memory_space=pl.ANY)] * len(held),
            out_specs=[spec, spec],
        ),
        out_shape=[shape, shape],
        input_output_aliases={count + 1: 0, count + 2: 1} if held else {},
        compiler_params=roomy(),
        cost_estimate=cost(0, 8 * count * depth * width),
    )(place, *blocks, *held)


def downdate_kernel(pieces, high, low, *refs):
    out, left_high, left_low = refs[-3:]
    count, _, width = pieces.shape

    @pl.when(pl.program_id(0) == 0)
    def _():
        for j in range(count):
            cut = slice(j * width, (j + 1) * width)
            left_high[:, cut], left_low[:, cut] = halves(pieces[j])

    total = three((left_high[...], left_low[...]), (high[0], low[0]), 0)
    for j in range(count):
        out[j] = total[j * width : (j + 1) * width]


def downdate_part(pieces, held, out, at):
    count, depth, width = pieces.shape
    wide = held[0].shape[2]
    rows = count * width
    specs = [pl.BlockSpec((count, depth, width), lambda j: (0, 0, 0))]
    specs += [pl.BlockSpec((1, depth, wide), lambda j: (j, 0, 0))] * 2
    ins = [pieces, *held]
    aliases = {}
    if out is not None:
        specs += [pl.BlockSpec(memory_space=pl.ANY)]
        ins += [out]
        aliases = {3: 0}
    return pl.pallas_call(
        downdate_kernel,
        grid=(8,),
        in_specs=specs,
        out_specs=pl.BlockSpec((count, width, wide), lambda j: (0, at, j)),
        out_shape=jax.ShapeDtypeStruct((count, wide, 8 * wide), jnp.float32),
        scratch_shapes=[pltpu.VMEM((depth, rows), jnp.bfloat16)] * 2,
        input_output_aliases=aliases,
        compiler_params=roomy(),
        cost_estimate=cost(
            6 * depth * rows * 8 * wide, 4 * (depth * rows + 8 * depth * wide + rows * 8 * wide)
        ),
    )(*ins)


CORE = [(i, i ^ 1) for i in range(8)]
ALONG_X = [(i, i ^ 2) for i in range(8)]
ALONG_Y = [(i, i ^ 4) for i in range(8)]


SAME_CORE = [[0, 2, 4, 6], [1, 3, 5, 7]]


def to_chips(blocks):
    return lax.all_to_all(blocks, "row", 0, 0, axis_index_groups=SAME_CORE)


def after(x, *others):
    return lax.optimization_barrier((x, *others))[0]


def local(factor_rows, prev_solution, cross_rows, inverses, coupling):
    rank, plane = lax.axis_index("row"), lax.axis_index("col")
    chip, core = rank // 2, rank % 2
    depth = 2 * factor_rows.shape[0]
    width = prev_solution.shape[1]
    half, quarter = width // 16, width // 32
    ints = lambda *values: jnp.stack([jnp.asarray(v, jnp.int32) for v in values])

    matrix = transfer_matrix(inverses, coupling)
    there = lambda x: lax.dynamic_slice_in_dim(
        x, (1 - core) * (width // 2), width // 2, x.ndim - 1
    )
    p_given = lax.ppermute(there(prev_solution), "row", CORE)
    c_own = jnp.swapaxes(cross_rows, 0, 1)
    c_given = lax.ppermute(there(c_own), "row", CORE)
    f_own = jnp.swapaxes(factor_rows, 0, 1).reshape(depth, -1)
    f_given = lax.ppermute(f_own, "row", CORE)
    sources = (f_own, f_given, prev_solution, p_given, c_own, c_given)

    away = (
        ((0, 0, 0, quarter), (1, 0, quarter, quarter)),
        ((2, 0, 0, quarter), (5, 0, quarter, quarter)),
        ((4, 0, 0, quarter), (3, 0, quarter, quarter)),
    )

    def updates(places, steps, widths):
        spots = [(chip ^ across) * 2 + side for across, side in places]
        return update_blocks(ints(*spots, core, rank, rank ^ 1), steps, widths, sources)

    shifted = tuple(tuple((out - 2, *rest) for out, *rest in step) for step in away[1:])
    early = updates(((3, 0),), away[:1], (quarter,) * 2)
    early += updates(((1, 0), (2, 0)), shifted, (quarter,) * 4)
    late = updates(((3, 1), (1, 1), (2, 1)), away, (quarter,) * 6)
    keep, late_keep = updates(
        ((0, 0), (0, 1)), (((0, 0, 0, half),), ((1, 0, 0, half),)), (half, half)
    )

    def passed(a_pass, b_pass):
        return lax.ppermute(a_pass, "row", ALONG_X), lax.ppermute(b_pass, "row", ALONG_Y)

    def arrivals(first, a_send, b_send, a_on, b_on):
        a_got, b_got = passed(a_send, b_send)
        a_last = lax.ppermute(a_on + first[0], "row", ALONG_Y)
        b_last = lax.ppermute(b_on + first[1], "row", ALONG_X)
        return a_got, b_got, a_last, b_last

    first = passed(*early[:2])
    first = after(first[0], late[0]), first[1]
    terms = arrivals(first, *early[2:])
    first = passed(*[after(x, terms[0]) for x in late[:2]])
    solved, chunk = solve(matrix, (keep, *terms), (half,), None)
    late_terms = arrivals(first, *late[2:])
    solved, late_half, *chunks = solve(
        matrix, (late_keep, *late_terms), (half, quarter, quarter), solved
    )
    blocks = [lax.all_gather(x, "col", axis=0) for x in (after(chunk, *first), *chunks)]

    x_early = lax.ppermute(after(chunk, late_half), "row", ALONG_X)
    y_late = lax.ppermute(late_half, "row", ALONG_Y)
    x_late = lax.ppermute(late_half, "row", ALONG_X)
    y_early = lax.ppermute(after(chunk, late_half), "row", ALONG_Y)
    twin = lax.ppermute(solved, "row", CORE)

    def split(blocks, pair, spots, held):
        places = [c * 4 + (chip ^ m) for c in (core, 1 - core) for m, _ in spots]
        sides = [side for _, side in spots] * 2
        return split_blocks(jnp.stack([ints(*places), ints(*sides)]), [*blocks, *pair], held)

    def given(*arrays):
        return [lax.ppermute(x, "row", CORE) for x in arrays]

    held = split([solved], [twin], ((0, 0),), ())
    first_chunk = blocks[0][:, :, :quarter]
    x_early, y_late = after(x_early, *held), after(y_late, *held)
    x_late, y_early = after(x_late, first_chunk), after(y_early, first_chunk)
    far_a = lax.ppermute(x_early, "row", ALONG_Y)
    far_b = lax.ppermute(y_late, "row", ALONG_X)
    sides = [x_early, x_late, y_early, y_late]
    held = split(sides, given(*sides), ((1, 0), (1, 1), (2, 0), (2, 1)), held)
    second_chunk = after(blocks[0], *held)[:, :, quarter:]
    far = jnp.concatenate([after(far_a, *held), far_b], axis=1)
    pieces = to_chips(first_chunk)
    twin = given(far)
    held = split([after(far, pieces, blocks[1])], twin, ((3, 0),), held)
    out = before = downdate_part(pieces, held, None, 0)
    pieces = to_chips(second_chunk)
    out = downdate_part(pieces, held, out, 1)
    pieces = to_chips(after(blocks[1], before))
    before, out = out, downdate_part(pieces, held, out, 2)
    pieces = to_chips(after(blocks[2], before))
    out = downdate_part(pieces, held, out, 3)
    return out.reshape(-1, width)


def local_any(factor_rows, prev_solution, cross_rows, inverses, coupling):
    full = lax.Precision.HIGHEST
    width = prev_solution.shape[1]
    fanout = lax.axis_size("row") // lax.axis_size("col")
    narrow = width // fanout
    rank = lax.axis_index("row")
    sums = lax.psum_scatter(
        jnp.einsum(
            "pks,sn->pkn",
            factor_rows,
            prev_solution,
            precision=full,
            preferred_element_type=jnp.float32,
        ),
        "row",
        scatter_dimension=0,
        tiled=True,
    )
    update = lax.all_gather(cross_rows - sums, "row", axis=0, tiled=True)
    lower = lax.all_gather(inverses, "row", axis=0, tiled=True)
    couple = lax.all_gather(coupling, "row", axis=0, tiled=True)
    first = dot(lower[:, 0, :], update[:, 0, :], full)
    rest = update[:, 1, :] - dot(couple, first, full)
    second = dot(lower[:, 1, :], rest, full)
    stacked = jnp.concatenate([first, second], axis=0)
    cut = lax.dynamic_slice_in_dim(stacked, rank % fanout * narrow, narrow, 1)
    mine = lax.axis_index("col") == rank // fanout
    picked = lax.psum(jnp.where(mine, cut, jnp.zeros_like(cut)), "col")
    return lax.dot_general(
        picked, stacked, (((0,), (0,)), ((), ())), precision=full, preferred_element_type=jnp.float32
    )


def solution(mesh):
    body = local if (mesh.shape["row"], mesh.shape["col"]) == (8, 4) else local_any
    return jax.shard_map(
        body,
        mesh=mesh,
        in_specs=(
            P(None, None, "row"),
            P("row", "col"),
            P("row", None, "col"),
            P("row", None, None),
            P("row", None),
        ),
        out_specs=P("row", "col"),
        check_vma=False,
    )
```
